256 devices in a mesh: grp: 8 (over y, x_lo), blk: 32 (over z, x_hi, core).
Axes of the slice: x: 4 (x_hi: 2, x_lo: 2; x = x_hi * 2 + x_lo), y: 4, z: 8, core: 2. Of those that a mesh axis runs over, the one named last changes fastest.
Arguments:
- amplitudes: float32 [8192, 128, 128], P('grp', 'blk'), may hold values from -6 to 6
- piece_len: int32 [128], P('blk'), may hold values from 32 to 128
- ladder_tiles: float32 [1024, 128, 128], P('blk'), may hold values from -0.03125 to 0.03125
- cycle_tiles: float32 [1024, 128, 128], P('blk'), may hold values from -0.03125 to 0.03125
- tile_owner: int32 [1024], replicated, may hold values from 0 to 31, as said below
- tile_piece: int32 [1024], replicated, may hold values from 0 to 3
- tile_block: int32 [1024], replicated, may hold values from 0 to 3
- pair_map: int32 [8, 32], replicated, may hold values from 0 to 7, as said below
Outputs:
- residual: float32 [8192, 512], P(('grp', 'blk'))
The draws below stay inside these ranges and needn't reach their ends.
Inputs may be any that keep to these rules, and one draw needn't show every extreme that they name: `tile_owner`: of the 32 tiles stored on one device along blk (tiles k * 32 to k * 32 + 31), at most 2 have the same owner; one owner has 2 tiles of every device. pair_map[g, s] is g XOR pair_map[0, s]; pair_map[0, s] is not 0 for at least one s.
All inputs are finite; a program needn't handle non-finite values.
Results may differ from the reference program's by a relative error of at most 0.00008.
Values sent between devices are 32-bit elements; how exact they have to be, the bound alone decides.
A program may use at most 320 MiB of HBM per device.

```python
import jax
import jax.numpy as jnp
from jax import lax

OPG = 1024
NT_DEV = 4
TW = 128
BW = 128
BLOCKS = 4
TILE_DEV = 32
PAIR_CAP = 2
OP = 8192
NT = 128
NTILE = 1024
N_GRP = 8
N_BLK = 32


def draw_tile_owner(key, part):
    key = jax.random.fold_in(key, 11)
    favored = jax.random.randint(jax.random.fold_in(key, 1), (), 0, N_BLK)
    others = jnp.arange((N_BLK - 1) * PAIR_CAP, dtype=jnp.int32) // PAIR_CAP
    keys = jax.random.split(jax.random.fold_in(key, 2), N_BLK)

    def one_block(sub):
        first, second = jax.random.split(sub)
        picked = jax.random.permutation(first, others)[:TILE_DEV - PAIR_CAP]
        picked = picked + (picked >= favored).astype(jnp.int32)
        row = jnp.concatenate([jnp.full((PAIR_CAP,), favored, jnp.int32), picked])
        return jax.random.permutation(second, row)
    return jax.vmap(one_block)(keys).reshape(-1).astype(jnp.int32)


def draw_pair_map(key, part):
    key = jax.random.fold_in(key, 23)
    offsets = jax.random.randint(jax.random.fold_in(key, 1), (N_BLK,), 0, N_GRP).astype(jnp.int32)
    chosen = jax.random.randint(jax.random.fold_in(key, 2), (), 0, N_BLK)
    forced = jax.random.randint(jax.random.fold_in(key, 3), (), 1, N_GRP).astype(jnp.int32)
    places = jnp.arange(N_BLK, dtype=jnp.int32)
    offsets = jnp.where(places == chosen, forced, offsets).astype(jnp.int32)
    groups = jnp.arange(N_GRP, dtype=jnp.int32)
    return jnp.bitwise_xor(groups[:, None], offsets[None, :]).astype(jnp.int32)


def with_ends(drawn, rng, low, high):
    longest = drawn.shape.index(max(drawn.shape))
    spots = []
    for shift in (0, 1):
        where = [jax.random.randint(jax.random.fold_in(rng, axis), (), 0, length) for axis, length in enumerate(drawn.shape)]
        where[longest] = (where[longest] + shift) % drawn.shape[longest]
        spots.append(tuple(where))
    return drawn.at[spots[0]].set(low).at[spots[1]].set(high)


def block_scale(stream_key, shape, cuts, smallest, top_value):
    loudness = 1.0
    for dim, parts in cuts:
        steps = jax.random.uniform(jax.random.fold_in(jax.random.fold_in(stream_key, 6), dim), (parts,), jnp.float32, smallest / len(cuts), top_value / len(cuts))
        loudness = loudness * jnp.repeat(jnp.exp(steps), shape[dim] // parts).reshape((-1,) + (1,) * (len(shape) - 1 - dim))
    return loudness


def noise(key, shape, spread, reach, pieces=(), held_as=jnp.bfloat16):
    values = jax.random.normal(key, shape, jnp.float32) * spread
    if len(pieces) > 0:
        values = block_scale(key, shape, pieces, -0.22, 0.18) * values
    return jnp.clip(values, min=-reach, max=reach).astype(held_as)


def setup_inputs(seed: int = 0) -> dict:
    key_list = jax.random.split(jax.random.key(seed), 9)
    return {
        "amplitudes": noise(key_list[0], (OP, NT, TW), 1.0, 6.0, ((0, 8), (1, 32)), jnp.float32),
        "piece_len": with_ends(jax.random.randint(key_list[1], (NT,), TW // 4, TW + 1), jax.random.fold_in(key_list[1], 1), TW // 4, TW).astype(jnp.int32),
        "ladder_tiles": noise(key_list[2], (NTILE, TW, BW), (NTILE * TW // BLOCKS) ** -0.5, 0.03125, ((0, 32),), jnp.float32),
        "cycle_tiles": noise(key_list[3], (NTILE, TW, BW), (NTILE * TW // BLOCKS) ** -0.5, 0.03125, ((0, 32),), jnp.float32),
        "tile_owner": draw_tile_owner(jax.random.fold_in(key_list[8], 71), 0),
        "tile_piece": with_ends(jax.random.randint(key_list[5], (NTILE,), 0, NT_DEV), jax.random.fold_in(key_list[5], 1), 0, NT_DEV - 1).astype(jnp.int32),
        "tile_block": with_ends(jax.random.randint(key_list[6], (NTILE,), 0, BLOCKS), jax.random.fold_in(key_list[6], 1), 0, BLOCKS - 1).astype(jnp.int32),
        "pair_map": draw_pair_map(jax.random.fold_in(key_list[8], 71), 0),
    }


def mirror_rows(field, pair_map):
    block_rows = OPG // N_BLK
    shaped = field.reshape((N_GRP, N_BLK, block_rows) + field.shape[1:])
    blocks = jnp.arange(N_BLK, dtype=jnp.int32)
    picked = shaped[pair_map, blocks[None, :]]
    return picked.reshape(field.shape)


def place_tiles(tiles, piece_ids, tile_block):
    big = jnp.zeros((NT, BLOCKS, TW, BW), jnp.float32)
    big = big.at[piece_ids, tile_block].add(tiles)
    return big.transpose(0, 2, 1, 3).reshape(NT * TW, BLOCKS * BW)


def reference(amplitudes, piece_len, ladder_tiles, cycle_tiles, tile_owner, tile_piece, tile_block, pair_map):
    columns = jnp.arange(TW, dtype=jnp.int32)
    keep = columns[None, :] < piece_len[:, None]
    masked = jnp.where(keep[None], amplitudes, 0.0)
    mirrored = mirror_rows(masked, pair_map)
    twiddled = 2.0 * masked - mirrored
    piece_ids = (tile_owner * NT_DEV + tile_piece).astype(jnp.int32)
    ladder = jnp.dot(masked.reshape(OP, NT * TW), place_tiles(ladder_tiles, piece_ids, tile_block),
                     precision=lax.Precision.HIGHEST, preferred_element_type=jnp.float32)
    cycle = jnp.dot(twiddled.reshape(OP, NT * TW), place_tiles(cycle_tiles, piece_ids, tile_block),
                   precision=lax.Precision.HIGHEST, preferred_element_type=jnp.float32)
    return ladder + cycle
```

```python
import functools

import jax
import jax.numpy as jnp
from jax import lax
from jax.experimental import pallas as pl
from jax.experimental.pallas import tpu as pltpu
from jax.sharding import PartitionSpec as P

BLOCKS = 4
PAIR_CAP = 2
F32 = jnp.float32
BF16 = jnp.bfloat16
I32 = jnp.int32

NZ = 8
NY = 4
N_BLK = 32
N_GRP = 8
TILES = 32
TW = 128
BW = 128
PIECES = 4
SL = TW // N_GRP
SLOT_ROWS = PAIR_CAP * SL
ROWS = 1024
BR = ROWS // N_BLK
KD = PIECES * TW
COLS = BLOCKS * BW


def iota(shape, dim):
    return lax.broadcasted_iota(I32, shape, dim)


def split2(x):
    hi = x.astype(BF16)
    lo = (x - hi.astype(F32)).astype(BF16)
    return hi, lo


def dot(a, b):
    return jnp.dot(a, b, preferred_element_type=F32)


def kernel(
    code_ref, codet_ref, pair_ref, plen_ref, amp_hbm, lad_hbm, cyc_hbm, out_ref,
    tl, cat, send, recv, w2, wh, wl, amp, ah, al, ps, po, pr, zh, zr, xr, bc, br, pres, kd,
    local_sem, a2a_send, a2a_recv, ag_send, ag_recv, core_send, core_recv,
    z_send, z_recv, x_send, x_recv, b_send, b_recv,
):
    me = lax.axis_index("blk")
    g = lax.axis_index("grp")
    z, xh, core = me // 4, (me // 2) % 2, me % 2
    y, xl = g // 2, g % 2

    def xor_grp(bit):
        return g + bit - 2 * bit * ((g // bit) % 2)

    def xor_blk(bit):
        return me + bit - 2 * bit * ((me // bit) % 2)

    def at_grp(dy, flip):
        return ((y + dy + NY) % NY) * 2 + (xl + flip) % 2

    def at_z(dz):
        return ((z + dz + NZ) % NZ) * 4 + me % 4

    rows = pl.ds(pl.multiple_of(g * SL, SL), SL)
    load_c = pltpu.make_async_copy(cyc_hbm.at[:, rows, :], tl.at[0], local_sem.at[0])
    load_l = pltpu.make_async_copy(lad_hbm.at[:, rows, :], tl.at[1], local_sem.at[1])
    load_a = pltpu.make_async_copy(amp_hbm, amp, local_sem.at[2])
    load_c.start()
    load_l.start()
    load_a.start()

    barrier = pltpu.get_barrier_semaphore()

    def greet(k, carry):
        pl.semaphore_signal(barrier, inc=1, device_id={"blk": (me + k) % N_BLK})
        return carry

    lax.fori_loop(1, N_BLK, greet, 0)
    for peer in (at_grp(0, 1), at_grp(1, 0), at_grp(-1, 0), at_grp(2, 0)):
        pl.semaphore_signal(barrier, inc=1, device_id={"grp": peer})

    own_r = code_ref[pl.ds(me, 1), :] // 16
    codet = codet_ref[...]
    owner_t = codet // 16
    own_c = jnp.sum(jnp.where(iota((TILES, N_BLK), 1) == me, owner_t, 0), axis=1, keepdims=True)
    same = jnp.where((own_c == own_r) & (iota((TILES, TILES), 0) < iota((TILES, TILES), 1)), 1, 0)
    slot = own_r * PAIR_CAP + jnp.sum(same, axis=0, keepdims=True)
    width = TILES * SL
    expand = jnp.where(iota((TILES, width), 1) // SL == iota((TILES, width), 0), 1.0, 0.0)
    slot8 = jnp.broadcast_to(slot.astype(F32), (8, TILES))
    slot_l = dot(slot8.astype(BF16), expand.astype(BF16))[0:1, :].astype(I32)
    goal = slot_l * SL + iota((1, width), 1) % SL

    def fill(st):
        hi, lo = split2(tl[st].reshape(width, BW))
        cat[:, :BW] = hi
        cat[:, BW:] = lo

        def block(b, carry):
            onehot = jnp.where(iota((128, width), 0) + b * 128 == goal, 1.0, 0.0).astype(BF16)
            both = dot(onehot, cat[...])
            send[st, pl.ds(pl.multiple_of(b * 128, 128), 128), :] = both[:, :BW] + both[:, BW:]
            return carry

        lax.fori_loop(0, N_BLK * SLOT_ROWS // 128, block, 0)

    def slot_rows(device):
        return pl.ds(pl.multiple_of(device * SLOT_ROWS, SLOT_ROWS), SLOT_ROWS)

    def spread(st):
        def one(k, carry):
            to = (me + k) % N_BLK
            pltpu.make_async_remote_copy(
                src_ref=send.at[st, slot_rows(to), :],
                dst_ref=recv.at[st, slot_rows(me), :],
                send_sem=a2a_send.at[st],
                recv_sem=a2a_recv.at[st],
                device_id={"blk": to},
            ).start()
            return carry

        lax.fori_loop(1, N_BLK, one, 0)
        recv[st, slot_rows(me), :] = send[st, slot_rows(me), :]

    def a2a_all(st, sem):
        part = recv.at[st, pl.ds(0, (N_BLK - 1) * SLOT_ROWS), :]
        return pltpu.make_async_copy(part, part, sem.at[st])

    load_c.wait()
    fill(0)
    pl.semaphore_wait(barrier, N_BLK - 1 + 4)
    spread(0)
    load_l.wait()
    fill(1)
    spread(1)

    hits = jnp.where(owner_t == me, 1.0, 0.0)
    tri = jnp.where(iota((TILES, TILES), 1) < iota((TILES, TILES), 0), 1.0, 0.0)
    before = dot(tri.astype(BF16), hits.astype(BF16))
    key = (codet % 16).astype(F32)
    depth = N_BLK * SLOT_ROWS
    key_l = jnp.zeros((8, depth), F32)
    for k in range(PAIR_CAP):
        chosen = jnp.where(before == float(k), hits, 0.0)
        found = jnp.sum(chosen, axis=0, keepdims=True)
        where = jnp.sum(chosen * key, axis=0, keepdims=True) + 64.0 * (1.0 - found)
        spots = jnp.where(iota((N_BLK, depth), 1) // SL == iota((N_BLK, depth), 0) * PAIR_CAP + k, 1.0, 0.0)
        key_l += dot(jnp.broadcast_to(where, (8, N_BLK)).astype(BF16), spots.astype(BF16))
    goal_d = key_l[0:1, :].astype(I32) * SL + iota((1, depth), 1) % SL
    for q in range(PIECES):
        kd[q] = jnp.where(iota((BLOCKS * SL, depth), 0) + q * BLOCKS * SL == goal_d, 1.0, 0.0).astype(BF16)

    def prepare(t, carry):
        for half in range(2):
            for p in range(PIECES):
                start = (t * 2 * BR + half * BR) * PIECES + p
                v = amp[pl.ds(start, BR, stride=PIECES), :]
                v = jnp.where(iota((BR, TW), 1) < plen_ref[p], v, 0.0)
                hi, lo = split2(v)
                r = pl.ds(pl.multiple_of(t * BR, BR), BR)
                ah[half, r, p * TW:(p + 1) * TW] = hi
                al[half, r, p * TW:(p + 1) * TW] = lo
        return carry

    load_a.wait()
    lax.fori_loop(0, N_BLK // 2, prepare, 0)

    def collect(st):
        a2a_all(st, a2a_recv).wait()
        hi, lo = split2(recv[st])
        for q in range(PIECES):
            total = dot(kd[q], hi) + dot(kd[q], lo)
            for b in range(BLOCKS):
                part = total[b * SL:(b + 1) * SL, :]
                cols = pl.ds(b * BW, BW)
                if st == 1:
                    part = part + 2.0 * w2[0, q, rows, cols]
                w2[st, q, rows, cols] = part

    def gather_copy(st, n, owner, part, to):
        at = pl.ds(pl.multiple_of(owner * SL, SL), SL)
        ref = w2.at[st, part, at, :]
        return pltpu.make_async_remote_copy(
            src_ref=ref, dst_ref=ref, send_sem=ag_send.at[st, n], recv_sem=ag_recv.at[st, n],
            device_id={"grp": to},
        )

    every, first, second = pl.ds(0, 4), pl.ds(0, 2), pl.ds(2, 2)
    up, down, side = at_grp(1, 0), at_grp(-1, 0), at_grp(0, 1)

    def sends(st, ns):
        table = {
            0: (g, every, side), 1: (g, every, up), 2: (g, every, down),
            3: (side, every, up), 4: (side, every, down),
            5: (down, first, up), 6: (up, second, down),
            7: (at_grp(-1, 1), first, up), 8: (at_grp(1, 1), second, down),
        }
        return [gather_copy(st, n, *table[n]) for n in ns]

    def arrivals(st, ns):
        table = {
            0: (side, every), 1: (down, every), 2: (up, every),
            3: (at_grp(-1, 1), every), 4: (at_grp(1, 1), every),
            5: (at_grp(2, 0), first), 6: (at_grp(2, 0), second),
            7: (at_grp(2, 1), first), 8: (at_grp(2, 1), second),
        }
        return [gather_copy(st, n, *table[n], side) for n in ns]

    def go(copies):
        for copy in copies:
            copy.start()

    def arrive(copies):
        for copy in copies:
            copy.wait_recv()

    def multiply(st):
        for q in range(PIECES):
            hi, lo = split2(w2[st, q])
            wh[q * TW:(q + 1) * TW, :] = hi
            wl[q * TW:(q + 1) * TW, :] = lo

        def product(half, dst):
            def tile(i, carry):
                r = pl.ds(pl.multiple_of(i * 256, 256), 256)
                a, b = ah[half, r, :], al[half, r, :]
                total = dot(a, wh[...]) + (dot(a, wl[...]) + dot(b, wh[...]))
                dst[st, r, :] = total
                return carry

            lax.fori_loop(0, 2, tile, 0)

        product(1 - core, ps)
        copy = core_copy(st)
        copy.start()
        product(core, po)

    def core_copy(st):
        return pltpu.make_async_remote_copy(
            src_ref=ps.at[st], dst_ref=pr.at[st], send_sem=core_send.at[st], recv_sem=core_recv.at[st],
            device_id={"blk": xor_blk(1)},
        )

    def core_add(st):
        core_copy(st).wait_recv()

        def one(i, carry):
            r = pl.ds(pl.multiple_of(i * 128, 128), 128)
            po[st, r, :] += pr[st, r, :]
            return carry

        lax.fori_loop(0, 4, one, 0)

    def chunk(d, half=None):
        base = ((d + NZ) % NZ) * 2 * BR
        if half is None:
            return pl.ds(pl.multiple_of(base, 2 * BR), 2 * BR)
        return pl.ds(pl.multiple_of(base + half * BR, BR), BR)

    def z_copy(st, way, j):
        d = z + 4 - j if way == 0 else z - 4 + j
        if j == 0:
            src, dst = po.at[st, chunk(d, way), :], zh.at[st, way]
        else:
            src, dst = po.at[st, chunk(d), :], zr.at[st, way, j - 1]
        return pltpu.make_async_remote_copy(
            src_ref=src, dst_ref=dst, send_sem=z_send.at[st, way, j], recv_sem=z_recv.at[st, way, j],
            device_id={"blk": at_z(1 if way == 0 else -1)},
        )

    def z_go(st, j):
        for way in range(2):
            if j > 0:
                z_take(st, way, j - 1)
            z_copy(st, way, j).start()

    def z_take(st, way, j):
        z_copy(st, way, j).wait_recv()
        d = z + 3 - j if way == 0 else z - 3 + j
        if j == 0:
            po[st, chunk(d, way), :] += zh[st, way]
        else:
            po[st, chunk(d), :] += zr[st, way, j - 1]

    def x_copy(st):
        return pltpu.make_async_remote_copy(
            src_ref=po.at[st, chunk(z, 1 - xh), :], dst_ref=xr.at[st],
            send_sem=x_send.at[st], recv_sem=x_recv.at[st], device_id={"blk": xor_blk(2)},
        )

    def x_go(st):
        z_take(st, 0, 3)
        z_take(st, 1, 3)
        x_copy(st).start()

    def x_take(st):
        x_copy(st).wait_recv()
        return po[st, chunk(z, xh), :] + xr[st]

    offset = pair_ref[g, me]

    def b_copy(b):
        return pltpu.make_async_remote_copy(
            src_ref=bc.at[b], dst_ref=br.at[b], send_sem=b_send.at[b], recv_sem=b_recv.at[b],
            device_id={"grp": xor_grp(1 << b)},
        )

    def b_take(b):
        b_copy(b).wait_recv()
        moved = (offset // (1 << b)) % 2 != (g // (1 << b)) % 2
        bc[b + 1] = jnp.where(moved, br[b], bc[b])

    collect(0)
    go(sends(0, (0, 1, 2)))
    arrive(arrivals(0, (0,)))
    go(sends(0, (3, 4)))
    arrive(arrivals(0, (1, 2)))
    go(sends(0, (5, 6)))
    arrive(arrivals(0, (3, 4)))
    go(sends(0, (7, 8)))
    arrive(arrivals(0, (5, 6, 7, 8)))
    multiply(0)
    collect(1)
    go(sends(1, (0, 1, 2)))
    core_add(0)
    z_go(0, 0)
    arrive(arrivals(1, (0,)))
    go(sends(1, (3, 4)))
    arrive(arrivals(1, (1, 2)))
    go(sends(1, (5, 6)))
    z_go(0, 1)
    arrive(arrivals(1, (3, 4)))
    go(sends(1, (7, 8)))
    z_go(0, 2)
    arrive(arrivals(1, (5, 6, 7, 8)))
    multiply(1)
    z_go(0, 3)
    core_add(1)
    z_go(1, 0)
    x_go(0)
    z_go(1, 1)
    bc[0] = x_take(0)
    b_copy(0).start()
    z_go(1, 2)
    b_take(0)
    b_copy(1).start()
    z_go(1, 3)
    b_take(1)
    b_copy(2).start()
    x_go(1)
    b_take(2)
    out_ref[...] = x_take(1) - bc[3]

    for st in range(2):
        a2a_all(st, a2a_send).wait()
        for copy in sends(st, range(9)):
            copy.wait_send()
        core_copy(st).wait_send()
        for way in range(2):
            for j in range(4):
                z_copy(st, way, j).wait_send()
        x_copy(st).wait_send()
    for b in range(3):
        b_copy(b).wait_send()


def shards(
    amplitudes, piece_len, ladder_tiles, cycle_tiles, tile_owner, tile_piece, tile_block, pair_map
):
    code = (tile_owner * 16 + tile_piece * 4 + tile_block).reshape(N_BLK, TILES)
    vmem, smem, anywhere = (
        pl.BlockSpec(memory_space=pltpu.VMEM),
        pl.BlockSpec(memory_space=pltpu.SMEM),
        pl.BlockSpec(memory_space=pl.ANY),
    )
    dma = pltpu.SemaphoreType.DMA
    return pl.pallas_call(
        kernel,
        out_shape=jax.ShapeDtypeStruct((BR, COLS), F32),
        in_specs=[vmem, vmem, smem, smem, anywhere, anywhere, anywhere],
        out_specs=vmem,
        scratch_shapes=[
            pltpu.VMEM((2, TILES, SL, BW), F32),
            pltpu.VMEM((TILES * SL, 2 * BW), BF16),
            pltpu.VMEM((2, N_BLK * SLOT_ROWS, BW), F32),
            pltpu.VMEM((2, N_BLK * SLOT_ROWS, BW), F32),
            pltpu.VMEM((2, PIECES, TW, COLS), F32),
            pltpu.VMEM((KD, COLS), BF16),
            pltpu.VMEM((KD, COLS), BF16),
            pltpu.VMEM((ROWS * PIECES, TW), F32),
            pltpu.VMEM((2, ROWS // 2, KD), BF16),
            pltpu.VMEM((2, ROWS // 2, KD), BF16),
            pltpu.VMEM((2, ROWS // 2, COLS), F32),
            pltpu.VMEM((2, ROWS // 2, COLS), F32),
            pltpu.VMEM((2, ROWS // 2, COLS), F32),
            pltpu.VMEM((2, 2, BR, COLS), F32),
            pltpu.VMEM((2, 2, 3, 2 * BR, COLS), F32),
            pltpu.VMEM((2, BR, COLS), F32),
            pltpu.VMEM((4, BR, COLS), F32),
            pltpu.VMEM((3, BR, COLS), F32),
            pltpu.VMEM((BR, COLS), F32),
            pltpu.VMEM((PIECES, BLOCKS * SL, N_BLK * SLOT_ROWS), BF16),
            dma((3,)),
            dma((2,)),
            dma((2,)),
            dma((2, 9)),
            dma((2, 9)),
            dma((2,)),
            dma((2,)),
            dma((2, 2, 4)),
            dma((2, 2, 4)),
            dma((2,)),
            dma((2,)),
            dma((3,)),
            dma((3,)),
        ],
        compiler_params=pltpu.CompilerParams(
            collective_id=0, has_side_effects=True, vmem_limit_bytes=40 * 1024 * 1024
        ),
    )(
        code, code.T, pair_map, piece_len,
        amplitudes.reshape(ROWS * PIECES, TW), ladder_tiles, cycle_tiles,
    )


def solution(mesh):
    placed = (
        P("grp", "blk", None),
        P("blk"),
        P("blk", None, None),
        P("blk", None, None),
        P(),
        P(),
        P(),
        P(),
    )
    return jax.shard_map(
        shards, mesh=mesh, in_specs=placed, out_specs=P(("grp", "blk"), None), check_vma=False
    )
```

```python
import functools

import jax
import jax.numpy as jnp
from jax import lax
from jax.experimental import pallas as pl
from jax.experimental.pallas import tpu as pltpu
from jax.sharding import PartitionSpec as P

BLOCKS = 4
PAIR_CAP = 2
F32 = jnp.float32
BF16 = jnp.bfloat16
I32 = jnp.int32

NZ = 8
NY = 4
N_BLK = 32
N_GRP = 8
TILES = 32
TW = 128
BW = 128
PIECES = 4
FIRST = 2
SL = TW // N_GRP
SLOT_ROWS = PAIR_CAP * SL
ROWS = 1024
BR = ROWS // N_BLK
KD = PIECES * TW
COLS = BLOCKS * BW


def iota(shape, dim):
    return lax.broadcasted_iota(I32, shape, dim)


def split2(x):
    hi = x.astype(BF16)
    lo = (x - hi.astype(F32)).astype(BF16)
    return hi, lo


def dot(a, b):
    return jnp.dot(a, b, preferred_element_type=F32)


def kernel(
    owner_hbm, piece_hbm, block_hbm, pair_hbm, plen_hbm, amp_hbm, lad_hbm, cyc_hbm, out_ref,
    maps, pair_ref, plen_ref, tl, cat, send, recv, w2, wh, wl, amp, ah, al, ps, po, pr, zr, xr, bc, br, kd,
    local_sem, a2a_send, a2a_recv, ag_send, ag_recv, core_send, core_recv,
    z_send, z_recv, x_send, x_recv, b_send, b_recv,
):
    me = lax.axis_index("blk")
    g = lax.axis_index("grp")
    z, xh, core = me // 4, (me // 2) % 2, me % 2
    y, xl = g // 2, g % 2

    def xor_grp(bit):
        return g + bit - 2 * bit * ((g // bit) % 2)

    def xor_blk(bit):
        return me + bit - 2 * bit * ((me // bit) % 2)

    def at_grp(dy, flip):
        return ((y + dy + NY) % NY) * 2 + (xl + flip) % 2

    def at_z(dz):
        return ((z + dz + NZ) % NZ) * 4 + me % 4

    rows = pl.ds(pl.multiple_of(g * SL, SL), SL)
    load_c = pltpu.make_async_copy(cyc_hbm.at[:, rows, :], tl.at[0], local_sem.at[0])
    load_l = pltpu.make_async_copy(lad_hbm.at[:, rows, :], tl.at[1], local_sem.at[1])
    load_a = pltpu.make_async_copy(amp_hbm, amp, local_sem.at[2])
    maps_in = [
        pltpu.make_async_copy(ref, maps.at[n], local_sem.at[3 + n])
        for n, ref in enumerate((owner_hbm, piece_hbm, block_hbm))
    ]
    load_pair = pltpu.make_async_copy(pair_hbm, pair_ref, local_sem.at[6])
    load_plen = pltpu.make_async_copy(plen_hbm, plen_ref, local_sem.at[7])
    for copy in maps_in:
        copy.start()
    load_c.start()
    load_l.start()
    load_plen.start()
    load_a.start()
    load_pair.start()
    started = []

    barrier = pltpu.get_barrier_semaphore()

    def greet(k, carry):
        pl.semaphore_signal(barrier, inc=1, device_id={"blk": (me + k) % N_BLK})
        return carry

    lax.fori_loop(1, N_BLK, greet, 0)
    for peer in (at_grp(0, 1), at_grp(1, 0), at_grp(-1, 0), at_grp(2, 0), at_grp(1, 1), at_grp(-1, 1)):
        pl.semaphore_signal(barrier, inc=1, device_id={"grp": peer})

    for copy in maps_in:
        copy.wait()
    lanes = N_BLK * TILES // 8
    per = lanes // TILES
    repeat = jnp.where(iota((N_BLK, 8), 0) // per == iota((N_BLK, 8), 1), 1.0, 0.0).astype(BF16)
    fold = jnp.where(iota((lanes, TILES), 0) % TILES == iota((lanes, TILES), 1), 1.0, 0.0).astype(BF16)
    mine = iota((N_BLK, lanes), 1) // TILES == iota((N_BLK, lanes), 0) % per

    def unfold(values):
        wide = jnp.where(mine, dot(repeat, values.astype(F32).astype(BF16)), 0.0)
        return dot(wide.astype(BF16), fold)

    owners = unfold(maps[0])
    keys = unfold(maps[1] * BLOCKS + maps[2])

    me_f = me.astype(F32)
    own_r = jnp.sum(jnp.where(iota((N_BLK, TILES), 0) == me, owners, 0.0), axis=0, keepdims=True)
    square = (TILES, TILES)
    own_c = jnp.sum(jnp.where(iota(square, 0) == iota(square, 1), own_r, 0.0), axis=1, keepdims=True)
    same = jnp.where((own_c == own_r) & (iota(square, 0) < iota(square, 1)), 1.0, 0.0)
    slot = own_r * PAIR_CAP + jnp.sum(same, axis=0, keepdims=True)
    width = TILES * SL
    expand = jnp.where(iota((TILES, width), 1) // SL == iota((TILES, width), 0), 1.0, 0.0)
    slot8 = jnp.broadcast_to(slot, (8, TILES))
    slot_l = dot(slot8.astype(BF16), expand.astype(BF16))[0:1, :].astype(I32)
    goal = slot_l * SL + iota((1, width), 1) % SL

    def fill(st):
        hi, lo = split2(tl[st].reshape(width, BW))
        cat[:, :BW] = hi
        cat[:, BW:] = lo

        def block(b, carry):
            onehot = jnp.where(iota((128, width), 0) + b * 128 == goal, 1.0, 0.0).astype(BF16)
            both = dot(onehot, cat[...])
            send[st, pl.ds(pl.multiple_of(b * 128, 128), 128), :] = both[:, :BW] + both[:, BW:]
            return carry

        lax.fori_loop(0, N_BLK * SLOT_ROWS // 128, block, 0)

    def slot_rows(device):
        return pl.ds(pl.multiple_of(device * SLOT_ROWS, SLOT_ROWS), SLOT_ROWS)

    def spread(st):
        def one(k, carry):
            to = (me + k) % N_BLK
            pltpu.make_async_remote_copy(
                src_ref=send.at[st, slot_rows(to), :],
                dst_ref=recv.at[st, slot_rows(me), :],
                send_sem=a2a_send.at[st],
                recv_sem=a2a_recv.at[st],
                device_id={"blk": to},
            ).start()
            return carry

        lax.fori_loop(1, N_BLK, one, 0)
        recv[st, slot_rows(me), :] = send[st, slot_rows(me), :]

    def a2a_all(st, sem):
        part = recv.at[st, pl.ds(0, (N_BLK - 1) * SLOT_ROWS), :]
        return pltpu.make_async_copy(part, part, sem.at[st])

    load_c.wait()
    fill(0)
    pl.semaphore_wait(barrier, N_BLK - 1 + 6)
    spread(0)
    load_l.wait()
    fill(1)
    spread(1)

    hits = jnp.where(owners == me_f, 1.0, 0.0)
    tri = jnp.where(iota(square, 0) < iota(square, 1), 1.0, 0.0)
    before = dot(hits.astype(BF16), tri.astype(BF16))
    depth = N_BLK * SLOT_ROWS
    place = iota((N_BLK, depth), 1) // SL - iota((N_BLK, depth), 0) * PAIR_CAP
    key_l = jnp.zeros((1, depth), F32)
    for k in range(PAIR_CAP):
        chosen = jnp.where(before == float(k), hits, 0.0)
        found = jnp.sum(chosen, axis=1, keepdims=True)
        where = jnp.sum(chosen * keys, axis=1, keepdims=True) + 64.0 * (1.0 - found)
        key_l += jnp.sum(jnp.where(place == k, where, 0.0), axis=0, keepdims=True)
    goal_d = key_l.astype(I32) * SL + iota((1, depth), 1) % SL
    for q in range(PIECES):
        kd[q] = jnp.where(iota((BLOCKS * SL, depth), 0) + q * BLOCKS * SL == goal_d, 1.0, 0.0).astype(BF16)

    def prepare(t, carry):
        source = (z + FIRST + t // 2 + NZ) % NZ * 2 + t % 2
        for half in range(2):
            for p in range(PIECES):
                start = (source * 2 * BR + half * BR) * PIECES + p
                v = amp[pl.ds(start, BR, stride=PIECES), :]
                v = jnp.where(iota((BR, TW), 1) < plen_ref[p], v, 0.0)
                hi, lo = split2(v)
                r = pl.ds(pl.multiple_of(t * BR, BR), BR)
                ah[half, r, p * TW:(p + 1) * TW] = hi
                al[half, r, p * TW:(p + 1) * TW] = lo
        return carry

    load_a.wait()
    load_plen.wait()
    lax.fori_loop(0, N_BLK // 2, prepare, 0)

    def collect(st):
        a2a_all(st, a2a_recv).wait()
        hi, lo = split2(recv[st])
        for q in range(PIECES):
            total = dot(kd[q], hi) + dot(kd[q], lo)
            for b in range(BLOCKS):
                part = total[b * SL:(b + 1) * SL, :]
                cols = pl.ds(b * BW, BW)
                if st == 1:
                    part = part + 2.0 * w2[0, q, rows, cols]
                w2[st, q, rows, cols] = part

    def gather_copy(st, n, owner, part, to):
        at = pl.ds(pl.multiple_of(owner * SL, SL), SL)
        ref = w2.at[st, part, at, :]
        return pltpu.make_async_remote_copy(
            src_ref=ref, dst_ref=ref, send_sem=ag_send.at[st, n], recv_sem=ag_recv.at[st, n],
            device_id={"grp": to},
        )

    every, first, second = pl.ds(0, 4), pl.ds(0, 2), pl.ds(2, 2)
    up, down, side = at_grp(1, 0), at_grp(-1, 0), at_grp(0, 1)

    def sends(st, ns):
        table = {
            0: (g, every, side), 1: (g, every, up), 2: (g, every, down),
            3: (g, every, at_grp(1, 1)), 4: (g, every, at_grp(-1, 1)),
            5: (down, first, up), 6: (up, second, down),
            7: (at_grp(-1, 1), first, up), 8: (at_grp(1, 1), second, down),
        }
        return [gather_copy(st, n, *table[n]) for n in ns]

    def arrivals(st, ns):
        table = {
            0: (side, every), 1: (down, every), 2: (up, every),
            3: (at_grp(-1, 1), every), 4: (at_grp(1, 1), every),
            5: (at_grp(2, 0), first), 6: (at_grp(2, 0), second),
            7: (at_grp(2, 1), first), 8: (at_grp(2, 1), second),
        }
        return [gather_copy(st, n, *table[n], side) for n in ns]

    def go(copies):
        for copy in copies:
            copy.start()
            started.append(copy)

    def arrive(copies):
        for copy in copies:
            copy.wait_recv()

    def widen(st):
        for q in range(PIECES):
            hi, lo = split2(w2[st, q])
            wh[q * TW:(q + 1) * TW, :] = hi
            wl[q * TW:(q + 1) * TW, :] = lo

    def product(st, half, dst, part):
        r = pl.ds(part * 256, 256)
        a, b = ah[half, r, :], al[half, r, :]
        dst[st, r, :] = dot(a, wh[...]) + (dot(a, wl[...]) + dot(b, wh[...]))

    def core_copy(st, part):
        r = pl.ds(part * 256, 256)
        return pltpu.make_async_remote_copy(
            src_ref=ps.at[st, r, :], dst_ref=pr.at[st, r, :],
            send_sem=core_send.at[st, part], recv_sem=core_recv.at[st, part],
            device_id={"blk": xor_blk(1)},
        )

    def core_add(st, part):
        core_copy(st, part).wait_recv()

        def one(i, carry):
            r = pl.ds(pl.multiple_of(part * 256 + i * 64, 64), 64)
            po[st, r, :] += pr[st, r, :]
            return carry

        lax.fori_loop(0, 4, one, 0)

    def multiply(st):
        widen(st)
        product(st, 1 - core, ps, 0)
        go([core_copy(st, 0)])
        product(st, 1 - core, ps, 1)
        go([core_copy(st, 1)])
        product(st, core, po, 0)
        core_add(st, 0)
        z_go(st, 0)
        product(st, core, po, 1)
        core_add(st, 1)

    def chunk(distance, half):
        return pl.ds(((distance - FIRST) % NZ * 2 + half) * BR, BR)

    def z_copy(st, way, half, j):
        distance = 4 - j if way == 0 else j - 4
        return pltpu.make_async_remote_copy(
            src_ref=po.at[st, chunk(distance, half), :], dst_ref=zr.at[st, way, half, j],
            send_sem=z_send.at[st, way, half, j], recv_sem=z_recv.at[st, way, half, j],
            device_id={"blk": at_z(1 if way == 0 else -1)},
        )

    def z_take(st, way, half, j):
        z_copy(st, way, half, j).wait_recv()
        distance = 3 - j if way == 0 else j - 3
        po[st, chunk(distance, half), :] += zr[st, way, half, j]

    def z_go(st, n):
        for lead in range(2):
            for way in range(2):
                half = way if lead == 0 else 1 - way
                j = n + lead
                if j > 3:
                    continue
                if n > 0:
                    z_take(st, way, half, j - 1)
                go([z_copy(st, way, half, j)])

    def own_rows(half):
        return pl.ds(pl.multiple_of(((NZ - FIRST) * 2 + half) * BR, BR), BR)

    def x_copy(st):
        return pltpu.make_async_remote_copy(
            src_ref=po.at[st, own_rows(1 - xh), :], dst_ref=xr.at[st],
            send_sem=x_send.at[st], recv_sem=x_recv.at[st], device_id={"blk": xor_blk(2)},
        )

    def x_go(st):
        for way in range(2):
            z_take(st, way, 1 - way, 3)
        for way in range(2):
            z_take(st, way, way, 3)
        go([x_copy(st)])

    def x_take(st):
        x_copy(st).wait_recv()
        return po[st, own_rows(xh), :] + xr[st]

    def b_copy(b):
        return pltpu.make_async_remote_copy(
            src_ref=bc.at[b], dst_ref=br.at[b], send_sem=b_send.at[b], recv_sem=b_recv.at[b],
            device_id={"grp": xor_grp(1 << b)},
        )

    def b_take(b):
        b_copy(b).wait_recv()
        if b == 0:
            load_pair.wait()
        offset = pair_ref[g, me]
        moved = (offset // (1 << b)) % 2 != (g // (1 << b)) % 2
        bc[b + 1] = jnp.where(moved, br[b], bc[b])

    collect(0)
    go(sends(0, (1, 2, 3, 4, 0)))
    arrive(arrivals(0, (1, 2)))
    go(sends(0, (5, 6)))
    arrive(arrivals(0, (3, 4)))
    go(sends(0, (7, 8)))
    arrive(arrivals(0, (0, 5, 6, 7, 8)))
    multiply(0)
    collect(1)
    go(sends(1, (1, 2, 3, 4, 0)))
    z_go(0, 1)
    arrive(arrivals(1, (1, 2)))
    go(sends(1, (5, 6)))
    z_go(0, 2)
    arrive(arrivals(1, (3, 4)))
    go(sends(1, (7, 8)))
    z_go(0, 3)
    arrive(arrivals(1, (0, 5, 6, 7, 8)))
    multiply(1)
    x_go(0)
    z_go(1, 1)
    bc[0] = x_take(0)
    go([b_copy(0)])
    z_go(1, 2)
    b_take(0)
    go([b_copy(1)])
    z_go(1, 3)
    b_take(1)
    go([b_copy(2)])
    x_go(1)
    b_take(2)
    out_ref[...] = x_take(1) - bc[3]

    for st in range(2):
        a2a_all(st, a2a_send).wait()
    for copy in started:
        copy.wait_send()


def shards(
    amplitudes, piece_len, ladder_tiles, cycle_tiles, tile_owner, tile_piece, tile_block, pair_map
):
    vmem, anywhere = pl.BlockSpec(memory_space=pltpu.VMEM), pl.BlockSpec(memory_space=pltpu.HBM)
    dma = pltpu.SemaphoreType.DMA
    return pl.pallas_call(
        kernel,
        out_shape=jax.ShapeDtypeStruct((BR, COLS), F32),
        in_specs=[anywhere] * 8,
        out_specs=vmem,
        scratch_shapes=[
            pltpu.VMEM((3, 8, N_BLK * TILES // 8), I32),
            pltpu.SMEM((N_GRP, N_BLK), I32),
            pltpu.SMEM((PIECES,), I32),
            pltpu.VMEM((2, TILES, SL, BW), F32),
            pltpu.VMEM((TILES * SL, 2 * BW), BF16),
            pltpu.VMEM((2, N_BLK * SLOT_ROWS, BW), F32),
            pltpu.VMEM((2, N_BLK * SLOT_ROWS, BW), F32),
            pltpu.VMEM((2, PIECES, TW, COLS), F32),
            pltpu.VMEM((KD, COLS), BF16),
            pltpu.VMEM((KD, COLS), BF16),
            pltpu.VMEM((ROWS * PIECES, TW), F32),
            pltpu.VMEM((2, ROWS // 2, KD), BF16),
            pltpu.VMEM((2, ROWS // 2, KD), BF16),
            pltpu.VMEM((2, ROWS // 2, COLS), F32),
            pltpu.VMEM((2, ROWS // 2, COLS), F32),
            pltpu.VMEM((2, ROWS // 2, COLS), F32),
            pltpu.VMEM((2, 2, 2, 4, BR, COLS), F32),
            pltpu.VMEM((2, BR, COLS), F32),
            pltpu.VMEM((4, BR, COLS), F32),
            pltpu.VMEM((3, BR, COLS), F32),
            pltpu.VMEM((PIECES, BLOCKS * SL, N_BLK * SLOT_ROWS), BF16),
            dma((8,)),
            dma((2,)),
            dma((2,)),
            dma((2, 9)),
            dma((2, 9)),
            dma((2, 2)),
            dma((2, 2)),
            dma((2, 2, 2, 4)),
            dma((2, 2, 2, 4)),
            dma((2,)),
            dma((2,)),
            dma((3,)),
            dma((3,)),
        ],
        compiler_params=pltpu.CompilerParams(
            collective_id=0, has_side_effects=True, vmem_limit_bytes=60 * 1024 * 1024
        ),
    )(
        tile_owner.reshape(8, -1), tile_piece.reshape(8, -1), tile_block.reshape(8, -1), pair_map, piece_len,
        amplitudes.reshape(ROWS * PIECES, TW), ladder_tiles, cycle_tiles,
    )


def solution(mesh):
    placed = (
        P("grp", "blk", None),
        P("blk"),
        P("blk", None, None),
        P("blk", None, None),
        P(),
        P(),
        P(),
        P(),
    )
    return jax.shard_map(
        shards, mesh=mesh, in_specs=placed, out_specs=P(("grp", "blk"), None), check_vma=False
    )
```

```python
import functools

import jax
import jax.numpy as jnp
from jax import lax
from jax.experimental import pallas as pl
from jax.experimental.pallas import tpu as pltpu
from jax.sharding import PartitionSpec as P

BLOCKS = 4
PAIR_CAP = 2
F32 = jnp.float32
BF16 = jnp.bfloat16
I32 = jnp.int32

NZ = 8
NY = 4
N_BLK = 32
N_GRP = 8
TILES = 32
TW = 128
BW = 128
PIECES = 4
FIRST = 2
PASSED = (0, 1)
STREAMS = 4
HALF = BW // 2
SL = TW // N_GRP
PK = SL // 2
SLOT_ROWS = PAIR_CAP * PK
ROWS = 1024
BR = ROWS // N_BLK
KD = PIECES * TW
COLS = BLOCKS * BW
SC = COLS // 2


def iota(shape, dim):
    return lax.broadcasted_iota(I32, shape, dim)


def split2(x):
    hi = x.astype(BF16)
    lo = (x - hi.astype(F32)).astype(BF16)
    return hi, lo


def interleave(a, b):
    left = lax.broadcasted_iota(I32, a.shape, 1) < HALF
    return jnp.where(left, a, pltpu.roll(b, HALF, 1)), jnp.where(left, pltpu.roll(a, HALF, 1), b)


def dot(a, b):
    return jnp.dot(a, b, preferred_element_type=F32)


def kernel(
    owner_hbm, piece_hbm, block_hbm, pair_hbm, plen_hbm, amp_hbm, lad_hbm, cyc_hbm, out_ref,
    maps, pair_ref, plen_ref, tl, cat, send, recv, w2, wh, wl, amp, ah, al, ps, po, pr, zr, xr, bc, br, kd,
    local_sem, a2a_send, a2a_recv, ag_send, ag_recv, core_send, core_recv,
    z_send, z_recv, x_send, x_recv, b_send, b_recv,
):
    me = lax.axis_index("blk")
    g = lax.axis_index("grp")
    z, xh, core = me // 4, (me // 2) % 2, me % 2
    y, xl = g // 2, g % 2

    def xor_grp(bit):
        return g + bit - 2 * bit * ((g // bit) % 2)

    def xor_blk(bit):
        return me + bit - 2 * bit * ((me // bit) % 2)

    def at_grp(dy, flip):
        return ((y + dy + NY) % NY) * 2 + (xl + flip) % 2

    def at_z(dz):
        return ((z + dz + NZ) % NZ) * 4 + me % 4

    rows = pl.ds(pl.multiple_of(g * SL, SL), SL)
    load_c = pltpu.make_async_copy(cyc_hbm.at[:, rows, :], tl.at[0], local_sem.at[0])
    load_l = pltpu.make_async_copy(lad_hbm.at[:, rows, :], tl.at[1], local_sem.at[1])
    load_a = pltpu.make_async_copy(amp_hbm, amp, local_sem.at[2])
    maps_in = [
        pltpu.make_async_copy(ref, maps.at[n], local_sem.at[3 + n])
        for n, ref in enumerate((owner_hbm, piece_hbm, block_hbm))
    ]
    load_pair = pltpu.make_async_copy(pair_hbm, pair_ref, local_sem.at[6])
    load_plen = pltpu.make_async_copy(plen_hbm, plen_ref, local_sem.at[7])
    for copy in maps_in:
        copy.start()
    load_c.start()
    load_l.start()
    load_plen.start()
    load_a.start()
    load_pair.start()
    started = []

    barrier = pltpu.get_barrier_semaphore()

    def greet(k, carry):
        pl.semaphore_signal(barrier, inc=1, device_id={"blk": (me + k) % N_BLK})
        return carry

    lax.fori_loop(1, N_BLK, greet, 0)
    for peer in [at_grp(dy, dx) for dy in range(4) for dx in range(2) if dy or dx]:
        pl.semaphore_signal(barrier, inc=1, device_id={"grp": peer})

    for copy in maps_in:
        copy.wait()
    lanes = N_BLK * TILES // 8
    per = lanes // TILES
    repeat = jnp.where(iota((N_BLK, 8), 0) // per == iota((N_BLK, 8), 1), 1.0, 0.0).astype(BF16)
    fold = jnp.where(iota((lanes, TILES), 0) % TILES == iota((lanes, TILES), 1), 1.0, 0.0).astype(BF16)
    mine = iota((N_BLK, lanes), 1) // TILES == iota((N_BLK, lanes), 0) % per

    def unfold(values):
        wide = jnp.where(mine, dot(repeat, values.astype(F32).astype(BF16)), 0.0)
        return dot(wide.astype(BF16), fold)

    owners = unfold(maps[0])
    keys = unfold(maps[1] * BLOCKS + maps[2])

    me_f = me.astype(F32)
    own_r = jnp.sum(jnp.where(iota((N_BLK, TILES), 0) == me, owners, 0.0), axis=0, keepdims=True)
    square = (TILES, TILES)
    own_c = jnp.sum(jnp.where(iota(square, 0) == iota(square, 1), own_r, 0.0), axis=1, keepdims=True)
    same = jnp.where((own_c == own_r) & (iota(square, 0) < iota(square, 1)), 1.0, 0.0)
    slot = own_r * PAIR_CAP + jnp.sum(same, axis=0, keepdims=True)
    width = TILES * PK
    expand = jnp.where(iota((TILES, width), 1) // PK == iota((TILES, width), 0), 1.0, 0.0)
    slot8 = jnp.broadcast_to(slot, (8, TILES))
    slot_l = dot(slot8.astype(BF16), expand.astype(BF16))[0:1, :].astype(I32)
    goal = slot_l * PK + iota((1, width), 1) % PK

    def fill(st):
        tiles = tl[st // 2]
        packed = interleave(tiles[:, :PK, :].reshape(width, BW), tiles[:, PK:, :].reshape(width, BW))
        hi, lo = split2(packed[st % 2])
        cat[:, :BW] = hi
        cat[:, BW:] = lo

        def block(b, carry):
            onehot = jnp.where(iota((128, width), 0) + b * 128 == goal, 1.0, 0.0).astype(BF16)
            both = dot(onehot, cat[...])
            send[st, pl.ds(pl.multiple_of(b * 128, 128), 128), :] = both[:, :BW] + both[:, BW:]
            return carry

        lax.fori_loop(0, N_BLK * SLOT_ROWS // 128, block, 0)

    def slot_rows(device):
        return pl.ds(pl.multiple_of(device * SLOT_ROWS, SLOT_ROWS), SLOT_ROWS)

    def spread_all(st):
        for hop_x in (1, 0):
            for hop_core in (0, 1):
                for hop in (4, 3, -3, 2, -2, 1, -1, 0):
                    if not (hop or hop_x or hop_core):
                        continue
                    to = (z + hop + NZ) % NZ * 4 + (xh + hop_x) % 2 * 2 + (core + hop_core) % 2
                    pltpu.make_async_remote_copy(
                        src_ref=send.at[st, slot_rows(to), :],
                        dst_ref=recv.at[st, slot_rows(me), :],
                        send_sem=a2a_send.at[st],
                        recv_sem=a2a_recv.at[st],
                        device_id={"blk": to},
                    ).start()

    def spread_wait(st):
        part = send.at[st, pl.ds(0, (N_BLK - 1) * SLOT_ROWS), :]
        pltpu.make_async_copy(part, part, a2a_send.at[st]).wait()

    def keep(st):
        recv[st, slot_rows(me), :] = send[st, slot_rows(me), :]

    def a2a_all(st):
        part = recv.at[st, pl.ds(0, (N_BLK - 1) * SLOT_ROWS), :]
        return pltpu.make_async_copy(part, part, a2a_recv.at[st])

    load_c.wait()
    fill(0)
    keep(0)
    pl.semaphore_wait(barrier, N_BLK - 1 + 7)
    spread_all(0)
    fill(1)
    keep(1)
    spread_all(1)
    load_l.wait()
    for st in (2, 3):
        fill(st)
        keep(st)
        spread_all(st)

    hits = jnp.where(owners == me_f, 1.0, 0.0)
    tri = jnp.where(iota(square, 0) < iota(square, 1), 1.0, 0.0)
    before = dot(hits.astype(BF16), tri.astype(BF16))
    depth = N_BLK * SLOT_ROWS
    place = iota((N_BLK, depth), 1) // PK - iota((N_BLK, depth), 0) * PAIR_CAP
    key_l = jnp.zeros((1, depth), F32)
    for k in range(PAIR_CAP):
        chosen = jnp.where(before == float(k), hits, 0.0)
        found = jnp.sum(chosen, axis=1, keepdims=True)
        where = jnp.sum(chosen * keys, axis=1, keepdims=True) + 64.0 * (1.0 - found)
        key_l += jnp.sum(jnp.where(place == k, where, 0.0), axis=0, keepdims=True)
    goal_d = key_l.astype(I32) * PK + iota((1, depth), 1) % PK
    kd[...] = jnp.where(iota((PIECES * BLOCKS * PK, depth), 0) == goal_d, 1.0, 0.0).astype(BF16)

    def prepare(t, carry):
        source = (z + FIRST + t // 2 + NZ) % NZ * 2 + t % 2
        for half in range(2):
            for p in range(PIECES):
                start = (source * 2 * BR + half * BR) * PIECES + p
                v = amp[pl.ds(start, BR, stride=PIECES), :]
                v = jnp.where(iota((BR, TW), 1) < plen_ref[p], v, 0.0)
                hi, lo = split2(v)
                r = pl.ds(pl.multiple_of(t * BR, BR), BR)
                ah[half, r, p * TW:(p + 1) * TW] = hi
                al[half, r, p * TW:(p + 1) * TW] = lo
        return carry

    load_a.wait()
    load_plen.wait()
    lax.fori_loop(0, N_BLK // 2, prepare, 0)

    def collect(st):
        a2a_all(st).wait()
        hi, lo = split2(recv[st])
        total = dot(kd[...], hi) + dot(kd[...], lo)
        for q in range(PIECES):
            for m in range(BLOCKS // 2):
                at = (q * BLOCKS + 2 * m) * PK
                part = jnp.concatenate(interleave(total[at:at + PK, :], total[at + PK:at + 2 * PK, :]), axis=0)
                cols = pl.ds(m * BW, BW)
                if st >= 2:
                    part = part + 2.0 * w2[st - 2, q, rows, cols]
                w2[st, q, rows, cols] = part

    def gather_copy(st, n, owner, to):
        at = pl.ds(pl.multiple_of(owner * SL, SL), SL)
        ref = w2.at[st, :, at, :]
        return pltpu.make_async_remote_copy(
            src_ref=ref, dst_ref=ref, send_sem=ag_send.at[st, n], recv_sem=ag_recv.at[st, n],
            device_id={"grp": to},
        )

    up, down, over, side = at_grp(1, 0), at_grp(-1, 0), at_grp(2, 0), at_grp(0, 1)
    up_side, down_side, over_side = at_grp(1, 1), at_grp(-1, 1), at_grp(2, 1)

    def sends(st, ns):
        table = {0: (g, side), 1: (g, up), 2: (g, down), 3: (g, over)}
        if st in PASSED:
            table.update({4: (side, up), 5: (side, down), 6: (side, over)})
        else:
            table.update({4: (g, up_side), 5: (g, down_side), 6: (g, over_side)})
        return [gather_copy(st, n, *table[n]) for n in ns]

    def arrivals(st, ns):
        table = {0: side, 1: down, 2: up, 3: over, 4: down_side, 5: up_side, 6: over_side}
        return [gather_copy(st, n, table[n], side) for n in ns]

    def go(copies):
        for copy in copies:
            copy.start()
            started.append(copy)

    def arrive(copies):
        for copy in copies:
            copy.wait_recv()

    def widen(st):
        for q in range(PIECES):
            hi, lo = split2(w2[st, q])
            wh[q * TW:(q + 1) * TW, :] = hi
            wl[q * TW:(q + 1) * TW, :] = lo

    def product(st, half, dst, part):
        r = pl.ds(part * 256, 256)
        a, b = ah[half, r, :], al[half, r, :]
        dst[st, r, :] = dot(a, wh[...]) + (dot(a, wl[...]) + dot(b, wh[...]))

    def core_copy(st, part):
        r = pl.ds(part * 256, 256)
        return pltpu.make_async_remote_copy(
            src_ref=ps.at[st, r, :], dst_ref=pr.at[st, r, :],
            send_sem=core_send.at[st, part], recv_sem=core_recv.at[st, part],
            device_id={"blk": xor_blk(1)},
        )

    def core_add(st, part):
        core_copy(st, part).wait_recv()

        def one(i, carry):
            r = pl.ds(pl.multiple_of(part * 256 + i * 64, 64), 64)
            po[st, r, :] += pr[st, r, :]
            return carry

        lax.fori_loop(0, 4, one, 0)

    def multiply(st):
        widen(st)
        product(st, 1 - core, ps, 0)
        go([core_copy(st, 0)])
        product(st, 1 - core, ps, 1)
        go([core_copy(st, 1)])
        product(st, core, po, 0)
        core_add(st, 0)
        z_go(st, 0)
        product(st, core, po, 1)
        core_add(st, 1)

    def chunk(distance, half):
        return pl.ds(((distance - FIRST) % NZ * 2 + half) * BR, BR)

    def z_copy(st, way, half, j):
        distance = 4 - j if way == 0 else j - 4
        return pltpu.make_async_remote_copy(
            src_ref=po.at[st, chunk(distance, half), :], dst_ref=zr.at[st, way, half, j],
            send_sem=z_send.at[st, way, half, j], recv_sem=z_recv.at[st, way, half, j],
            device_id={"blk": at_z(1 if way == 0 else -1)},
        )

    def z_take(st, way, half, j):
        z_copy(st, way, half, j).wait_recv()
        distance = 3 - j if way == 0 else j - 3
        po[st, chunk(distance, half), :] += zr[st, way, half, j]

    def z_go(st, n):
        for lead in range(2):
            for way in range(2):
                half = way if lead == 0 else 1 - way
                j = n + lead
                if j > 3:
                    continue
                if n > 0:
                    z_take(st, way, half, j - 1)
                go([z_copy(st, way, half, j)])

    def own_rows(half):
        return pl.ds(pl.multiple_of(((NZ - FIRST) * 2 + half) * BR, BR), BR)

    def x_copy(st):
        return pltpu.make_async_remote_copy(
            src_ref=po.at[st, own_rows(1 - xh), :], dst_ref=xr.at[st],
            send_sem=x_send.at[st], recv_sem=x_recv.at[st], device_id={"blk": xor_blk(2)},
        )

    def x_go(st):
        for way in range(2):
            z_take(st, way, 1 - way, 3)
        for way in range(2):
            z_take(st, way, way, 3)
        go([x_copy(st)])

    def x_take(st):
        x_copy(st).wait_recv()
        return po[st, own_rows(xh), :] + xr[st]

    def b_copy(st, b):
        return pltpu.make_async_remote_copy(
            src_ref=bc.at[st, b], dst_ref=br.at[st, b], send_sem=b_send.at[st, b], recv_sem=b_recv.at[st, b],
            device_id={"grp": xor_grp(1 << b)},
        )

    def b_take(st, b):
        b_copy(st, b).wait_recv()
        moved = (pair_ref[g, me] // (1 << b)) % 2 != (g // (1 << b)) % 2
        bc[st, b + 1] = jnp.where(moved, br[st, b], bc[st, b])

    def gather_first(st):
        collect(st)
        go(sends(st, (0, 1, 2, 3) if st in PASSED else (6, 3, 4, 5, 1, 2, 0)))

    def gather_side(st):
        arrive(arrivals(st, (0,)))
        go(sends(st, (6, 4, 5)))

    def gather_last(st):
        arrive(arrivals(st, range(1 if st in PASSED else 0, 7)))
        multiply(st)

    def mirror(st, b):
        if b == 0:
            if st == 0:
                load_pair.wait()
            bc[st, 0] = x_take(st)
        else:
            b_take(st, b - 1)
        if b < 3:
            go([b_copy(st, b)])

    ring = [functools.partial(z_go, n=n) for n in range(1, 4)] + [x_go]
    ring += [functools.partial(mirror, b=b) for b in range(4)]
    passed_at = (0, 3.5, 9, 14.5, 17.5, 20.5, 23.5, 27, 30.5, 34, 37.5)
    direct_at = (0, 8, 13.5, 16.5, 19.5, 22.5, 26, 29.5, 33, 36.5)
    steps = []
    for st in range(STREAMS):
        if st in PASSED:
            chain, after = [gather_first, gather_side, gather_last] + ring, passed_at
        else:
            chain, after = [gather_first, gather_last] + ring, direct_at
        if st >= 2:
            chain = chain[:-4]
        steps += [(7.5 + 5.7 * st + at, st, step) for at, step in zip(after, chain)]
    for _, st, step in sorted(steps, key=lambda item: item[:2]):
        step(st)
    halves = [x_take(2 + h) - bc[h, 3] for h in range(2)]
    for m in range(BLOCKS // 2):
        cols = slice(m * BW, (m + 1) * BW)
        pair = interleave(halves[0][:, cols], halves[1][:, cols])
        for n in range(2):
            out_ref[:, (2 * m + n) * BW:(2 * m + n + 1) * BW] = pair[n]

    for st in range(STREAMS):
        spread_wait(st)
    for copy in started:
        copy.wait_send()


def shards(
    amplitudes, piece_len, ladder_tiles, cycle_tiles, tile_owner, tile_piece, tile_block, pair_map
):
    vmem, anywhere = pl.BlockSpec(memory_space=pltpu.VMEM), pl.BlockSpec(memory_space=pltpu.HBM)
    dma = pltpu.SemaphoreType.DMA
    return pl.pallas_call(
        kernel,
        out_shape=jax.ShapeDtypeStruct((BR, COLS), F32),
        in_specs=[anywhere] * 8,
        out_specs=vmem,
        scratch_shapes=[
            pltpu.VMEM((3, 8, N_BLK * TILES // 8), I32),
            pltpu.SMEM((N_GRP, N_BLK), I32),
            pltpu.SMEM((PIECES,), I32),
            pltpu.VMEM((2, TILES, SL, BW), F32),
            pltpu.VMEM((TILES * PK, 2 * BW), BF16),
            pltpu.VMEM((STREAMS, N_BLK * SLOT_ROWS, BW), F32),
            pltpu.VMEM((STREAMS, N_BLK * SLOT_ROWS, BW), F32),
            pltpu.VMEM((STREAMS, PIECES, TW, SC), F32),
            pltpu.VMEM((KD, SC), BF16),
            pltpu.VMEM((KD, SC), BF16),
            pltpu.VMEM((ROWS * PIECES, TW), F32),
            pltpu.VMEM((2, ROWS // 2, KD), BF16),
            pltpu.VMEM((2, ROWS // 2, KD), BF16),
            pltpu.VMEM((STREAMS, ROWS // 2, SC), F32),
            pltpu.VMEM((STREAMS, ROWS // 2, SC), F32),
            pltpu.VMEM((STREAMS, ROWS // 2, SC), F32),
            pltpu.VMEM((STREAMS, 2, 2, 4, BR, SC), F32),
            pltpu.VMEM((STREAMS, BR, SC), F32),
            pltpu.VMEM((2, 4, BR, SC), F32),
            pltpu.VMEM((2, 3, BR, SC), F32),
            pltpu.VMEM((PIECES * BLOCKS * PK, N_BLK * SLOT_ROWS), BF16),
            dma((8,)),
            dma((STREAMS,)),
            dma((STREAMS,)),
            dma((STREAMS, 9)),
            dma((STREAMS, 9)),
            dma((STREAMS, 2)),
            dma((STREAMS, 2)),
            dma((STREAMS, 2, 2, 4)),
            dma((STREAMS, 2, 2, 4)),
            dma((STREAMS,)),
            dma((STREAMS,)),
            dma((2, 3)),
            dma((2, 3)),
        ],
        compiler_params=pltpu.CompilerParams(
            collective_id=0, has_side_effects=True, vmem_limit_bytes=60 * 1024 * 1024
        ),
    )(
        tile_owner.reshape(8, -1), tile_piece.reshape(8, -1), tile_block.reshape(8, -1), pair_map, piece_len,
        amplitudes.reshape(ROWS * PIECES, TW), ladder_tiles, cycle_tiles,
    )


def solution(mesh):
    placed = (
        P("grp", "blk", None),
        P("blk"),
        P("blk", None, None),
        P("blk", None, None),
        P(),
        P(),
        P(),
        P(),
    )
    return jax.shard_map(
        shards, mesh=mesh, in_specs=placed, out_specs=P(("grp", "blk"), None), check_vma=False
    )
```

```python
import functools

import jax
import jax.numpy as jnp
from jax import lax
from jax.experimental import pallas as pl
from jax.experimental.pallas import tpu as pltpu
from jax.sharding import PartitionSpec as P

BLOCKS = 4
PAIR_CAP = 2
F32 = jnp.float32
BF16 = jnp.bfloat16
I32 = jnp.int32

NZ = 8
NY = 4
N_BLK = 32
N_GRP = 8
TILES = 32
TW = 128
BW = 128
PIECES = 4
FIRST = 2
PASSED = (0, 1)
STREAMS = 4
HALF = BW // 2
SL = TW // N_GRP
PK = SL // 2
SLOT_ROWS = PAIR_CAP * PK
ROWS = 1024
BR = ROWS // N_BLK
KD = PIECES * TW
COLS = BLOCKS * BW
SC = COLS // 2


def iota(shape, dim):
    return lax.broadcasted_iota(I32, shape, dim)


def split2(x):
    hi = x.astype(BF16)
    lo = (x - hi.astype(F32)).astype(BF16)
    return hi, lo


def interleave(a, b):
    left = lax.broadcasted_iota(I32, a.shape, 1) < HALF
    return jnp.where(left, a, pltpu.roll(b, HALF, 1)), jnp.where(left, pltpu.roll(a, HALF, 1), b)


def dot(a, b):
    return jnp.dot(a, b, preferred_element_type=F32)


def kernel(
    owner_hbm, piece_hbm, block_hbm, pair_hbm, plen_hbm, amp_hbm, lad_hbm, cyc_hbm, out_ref,
    maps, pair_ref, plen_ref, tl, cat, send, recv, w2, wh, wl, amp, ah, al, ps, po, pr, zr, xr, bc, br, kd,
    local_sem, a2a_send, a2a_recv, ag_send, ag_recv, core_send, core_recv,
    z_send, z_recv, x_send, x_recv, b_send, b_recv,
):
    me = lax.axis_index("blk")
    g = lax.axis_index("grp")
    z, xh, core = me // 4, (me // 2) % 2, me % 2
    y, xl = g // 2, g % 2

    def xor_grp(bit):
        return g + bit - 2 * bit * ((g // bit) % 2)

    def xor_blk(bit):
        return me + bit - 2 * bit * ((me // bit) % 2)

    def at_grp(dy, flip):
        return ((y + dy + NY) % NY) * 2 + (xl + flip) % 2

    def at_z(dz):
        return ((z + dz + NZ) % NZ) * 4 + me % 4

    rows = pl.ds(pl.multiple_of(g * SL, SL), SL)
    load_c = pltpu.make_async_copy(cyc_hbm.at[:, rows, :], tl.at[0], local_sem.at[0])
    load_l = pltpu.make_async_copy(lad_hbm.at[:, rows, :], tl.at[1], local_sem.at[1])
    load_a = pltpu.make_async_copy(amp_hbm, amp, local_sem.at[2])
    maps_in = [
        pltpu.make_async_copy(ref, maps.at[n], local_sem.at[3 + n])
        for n, ref in enumerate((owner_hbm, piece_hbm, block_hbm))
    ]
    load_pair = pltpu.make_async_copy(pair_hbm, pair_ref, local_sem.at[6])
    load_plen = pltpu.make_async_copy(plen_hbm, plen_ref, local_sem.at[7])
    for copy in maps_in:
        copy.start()
    load_c.start()
    load_l.start()
    load_plen.start()
    load_a.start()
    load_pair.start()
    started = []

    barrier = pltpu.get_barrier_semaphore()

    def greet(k, carry):
        pl.semaphore_signal(barrier, inc=1, device_id={"blk": (me + k) % N_BLK})
        return carry

    lax.fori_loop(1, N_BLK, greet, 0)
    for peer in [at_grp(dy, dx) for dy in range(4) for dx in range(2) if dy or dx]:
        pl.semaphore_signal(barrier, inc=1, device_id={"grp": peer})

    for copy in maps_in:
        copy.wait()
    lanes = N_BLK * TILES // 8
    per = lanes // TILES
    repeat = jnp.where(iota((N_BLK, 8), 0) // per == iota((N_BLK, 8), 1), 1.0, 0.0).astype(BF16)
    fold = jnp.where(iota((lanes, TILES), 0) % TILES == iota((lanes, TILES), 1), 1.0, 0.0).astype(BF16)
    mine = iota((N_BLK, lanes), 1) // TILES == iota((N_BLK, lanes), 0) % per

    def unfold(values):
        wide = jnp.where(mine, dot(repeat, values.astype(F32).astype(BF16)), 0.0)
        return dot(wide.astype(BF16), fold)

    owners = unfold(maps[0])
    keys = unfold(maps[1] * BLOCKS + maps[2])

    me_f = me.astype(F32)
    own_r = jnp.sum(jnp.where(iota((N_BLK, TILES), 0) == me, owners, 0.0), axis=0, keepdims=True)
    square = (TILES, TILES)
    own_c = jnp.sum(jnp.where(iota(square, 0) == iota(square, 1), own_r, 0.0), axis=1, keepdims=True)
    same = jnp.where((own_c == own_r) & (iota(square, 0) < iota(square, 1)), 1.0, 0.0)
    slot = own_r * PAIR_CAP + jnp.sum(same, axis=0, keepdims=True)
    width = TILES * PK
    expand = jnp.where(iota((TILES, width), 1) // PK == iota((TILES, width), 0), 1.0, 0.0)
    slot8 = jnp.broadcast_to(slot, (8, TILES))
    slot_l = dot(slot8.astype(BF16), expand.astype(BF16))[0:1, :].astype(I32)
    goal = slot_l * PK + iota((1, width), 1) % PK

    def fill(st):
        tiles = tl[st // 2]
        packed = interleave(tiles[:, :PK, :].reshape(width, BW), tiles[:, PK:, :].reshape(width, BW))
        hi, lo = split2(packed[st % 2])
        cat[:, :BW] = hi
        cat[:, BW:] = lo

        def block(b, carry):
            onehot = jnp.where(iota((128, width), 0) + b * 128 == goal, 1.0, 0.0).astype(BF16)
            both = dot(onehot, cat[...])
            send[st, pl.ds(pl.multiple_of(b * 128, 128), 128), :] = both[:, :BW] + both[:, BW:]
            return carry

        lax.fori_loop(0, N_BLK * SLOT_ROWS // 128, block, 0)

    def slot_rows(device):
        return pl.ds(pl.multiple_of(device * SLOT_ROWS, SLOT_ROWS), SLOT_ROWS)

    def spread_all(st):
        for hop_x in (1, 0):
            for hop_core in (0, 1):
                for hop in (4, 3, -3, 2, -2, 1, -1, 0):
                    if not (hop or hop_x or hop_core):
                        continue
                    to = (z + hop + NZ) % NZ * 4 + (xh + hop_x) % 2 * 2 + (core + hop_core) % 2
                    pltpu.make_async_remote_copy(
                        src_ref=send.at[st, slot_rows(to), :],
                        dst_ref=recv.at[st, slot_rows(me), :],
                        send_sem=a2a_send.at[st],
                        recv_sem=a2a_recv.at[st],
                        device_id={"blk": to},
                    ).start()

    def spread_wait(st):
        part = send.at[st, pl.ds(0, (N_BLK - 1) * SLOT_ROWS), :]
        pltpu.make_async_copy(part, part, a2a_send.at[st]).wait()

    def keep(st):
        recv[st, slot_rows(me), :] = send[st, slot_rows(me), :]

    def a2a_all(st):
        part = recv.at[st, pl.ds(0, (N_BLK - 1) * SLOT_ROWS), :]
        return pltpu.make_async_copy(part, part, a2a_recv.at[st])

    load_c.wait()
    fill(0)
    keep(0)
    pl.semaphore_wait(barrier, N_BLK - 1 + 7)
    spread_all(0)
    fill(1)
    keep(1)
    spread_all(1)
    load_l.wait()
    for st in (2, 3):
        fill(st)
        keep(st)
        spread_all(st)

    hits = jnp.where(owners == me_f, 1.0, 0.0)
    tri = jnp.where(iota(square, 0) < iota(square, 1), 1.0, 0.0)
    before = dot(hits.astype(BF16), tri.astype(BF16))
    depth = N_BLK * SLOT_ROWS
    place = iota((N_BLK, depth), 1) // PK - iota((N_BLK, depth), 0) * PAIR_CAP
    key_l = jnp.zeros((1, depth), F32)
    for k in range(PAIR_CAP):
        chosen = jnp.where(before == float(k), hits, 0.0)
        found = jnp.sum(chosen, axis=1, keepdims=True)
        where = jnp.sum(chosen * keys, axis=1, keepdims=True) + 64.0 * (1.0 - found)
        key_l += jnp.sum(jnp.where(place == k, where, 0.0), axis=0, keepdims=True)
    goal_d = key_l.astype(I32) * PK + iota((1, depth), 1) % PK
    kd[...] = jnp.where(iota((PIECES * BLOCKS * PK, depth), 0) == goal_d, 1.0, 0.0).astype(BF16)

    def prepare(t, carry):
        source = (z + FIRST + t // 2 + NZ) % NZ * 2 + t % 2
        for half in range(2):
            for p in range(PIECES):
                start = (source * 2 * BR + half * BR) * PIECES + p
                v = amp[pl.ds(start, BR, stride=PIECES), :]
                v = jnp.where(iota((BR, TW), 1) < plen_ref[p], v, 0.0)
                hi, lo = split2(v)
                r = pl.ds(pl.multiple_of(t * BR, BR), BR)
                ah[half, r, p * TW:(p + 1) * TW] = hi
                al[half, r, p * TW:(p + 1) * TW] = lo
        return carry

    load_a.wait()
    load_plen.wait()
    lax.fori_loop(0, N_BLK // 2, prepare, 0)

    def collect(st):
        a2a_all(st).wait()
        hi, lo = split2(recv[st])
        total = dot(kd[...], hi) + dot(kd[...], lo)
        for q in range(PIECES):
            for m in range(BLOCKS // 2):
                at = (q * BLOCKS + 2 * m) * PK
                part = jnp.concatenate(interleave(total[at:at + PK, :], total[at + PK:at + 2 * PK, :]), axis=0)
                cols = pl.ds(m * BW, BW)
                if st >= 2:
                    part = part + 2.0 * w2[st - 2, q, rows, cols]
                w2[st, q, rows, cols] = part

    def gather_copy(st, n, owner, to):
        at = pl.ds(pl.multiple_of(owner * SL, SL), SL)
        ref = w2.at[st, :, at, :]
        return pltpu.make_async_remote_copy(
            src_ref=ref, dst_ref=ref, send_sem=ag_send.at[st, n], recv_sem=ag_recv.at[st, n],
            device_id={"grp": to},
        )

    up, down, over, side = at_grp(1, 0), at_grp(-1, 0), at_grp(2, 0), at_grp(0, 1)
    up_side, down_side, over_side = at_grp(1, 1), at_grp(-1, 1), at_grp(2, 1)

    def sends(st, ns):
        table = {0: (g, side), 1: (g, up), 2: (g, down), 3: (g, over)}
        if st in PASSED:
            table.update({4: (side, up), 5: (side, down), 6: (side, over)})
        else:
            table.update({4: (g, up_side), 5: (g, down_side), 6: (g, over_side)})
        return [gather_copy(st, n, *table[n]) for n in ns]

    def arrivals(st, ns):
        table = {0: side, 1: down, 2: up, 3: over, 4: down_side, 5: up_side, 6: over_side}
        return [gather_copy(st, n, table[n], side) for n in ns]

    def go(copies):
        for copy in copies:
            copy.start()
            started.append(copy)

    def arrive(copies):
        for copy in copies:
            copy.wait_recv()

    def widen(st):
        for q in range(PIECES):
            hi, lo = split2(w2[st, q])
            wh[q * TW:(q + 1) * TW, :] = hi
            wl[q * TW:(q + 1) * TW, :] = lo

    def product(st, half, dst, part):
        r = pl.ds(part * 256, 256)
        a, b = ah[half, r, :], al[half, r, :]
        dst[st, r, :] = dot(a, wh[...]) + (dot(a, wl[...]) + dot(b, wh[...]))

    def core_copy(st, part):
        r = pl.ds(part * 256, 256)
        return pltpu.make_async_remote_copy(
            src_ref=ps.at[st, r, :], dst_ref=pr.at[st, r, :],
            send_sem=core_send.at[st, part], recv_sem=core_recv.at[st, part],
            device_id={"blk": xor_blk(1)},
        )

    def core_add(st, part):
        core_copy(st, part).wait_recv()

        def one(i, carry):
            r = pl.ds(pl.multiple_of(part * 256 + i * 64, 64), 64)
            po[st, r, :] += pr[st, r, :]
            return carry

        lax.fori_loop(0, 4, one, 0)

    def multiply(st):
        widen(st)
        product(st, 1 - core, ps, 0)
        go([core_copy(st, 0)])
        product(st, 1 - core, ps, 1)
        go([core_copy(st, 1)])
        product(st, core, po, 0)
        core_add(st, 0)
        z_far(st)
        product(st, core, po, 1)
        core_add(st, 1)
        z_near(st)

    def chunk(distance, half):
        return pl.ds(((distance - FIRST) % NZ * 2 + half) * BR, BR)

    def z_copy(st, way, half, distance):
        sign = 1 - 2 * way
        return pltpu.make_async_remote_copy(
            src_ref=po.at[st, chunk(sign * distance, half), :], dst_ref=zr.at[st, way, half, distance - 1],
            send_sem=z_send.at[st, way, half, distance - 1], recv_sem=z_recv.at[st, way, half, distance - 1],
            device_id={"blk": at_z(sign * (1 if distance % 2 else 2))},
        )

    def z_far(st):
        for way in range(2):
            go([z_copy(st, way, way, 4)])
        for half in range(2):
            for way in range(2):
                go([z_copy(st, way, half, 3)])

    def z_near(st):
        for half in range(2):
            for way in range(2):
                go([z_copy(st, way, half, 1)])

    def z_mid(st):
        for lead in (1, 0):
            for way in range(2):
                half = way if lead == 0 else 1 - way
                z_copy(st, way, half, 3).wait_recv()
                total = po[st, chunk(2 - 4 * way, half), :] + zr[st, way, half, 2]
                if lead == 0:
                    z_copy(st, way, half, 4).wait_recv()
                    total = total + zr[st, way, half, 3]
                po[st, chunk(2 - 4 * way, half), :] = total
                go([z_copy(st, way, half, 2)])

    def own_rows(half):
        return pl.ds(pl.multiple_of(((NZ - FIRST) * 2 + half) * BR, BR), BR)

    def x_copy(st):
        return pltpu.make_async_remote_copy(
            src_ref=po.at[st, own_rows(1 - xh), :], dst_ref=xr.at[st],
            send_sem=x_send.at[st], recv_sem=x_recv.at[st], device_id={"blk": xor_blk(2)},
        )

    def finish(st, half):
        for distance in (1, 2):
            for way in range(2):
                part = zr.at[st, way, half, distance - 1]
                pltpu.make_async_copy(part, part, z_recv.at[st, way, half, distance - 1]).wait()
        near = zr[st, 0, half, 0] + zr[st, 1, half, 0]
        po[st, own_rows(half), :] += near + (zr[st, 0, half, 1] + zr[st, 1, half, 1])

    def x_go(st):
        finish(st, 1 - xh)
        go([x_copy(st)])
        finish(st, xh)

    def x_take(st):
        x_copy(st).wait_recv()
        return po[st, own_rows(xh), :] + xr[st]

    def b_copy(st, b):
        return pltpu.make_async_remote_copy(
            src_ref=bc.at[st, b], dst_ref=br.at[st, b], send_sem=b_send.at[st, b], recv_sem=b_recv.at[st, b],
            device_id={"grp": xor_grp(1 << b)},
        )

    def b_take(st, b):
        b_copy(st, b).wait_recv()
        moved = (pair_ref[g, me] // (1 << b)) % 2 != (g // (1 << b)) % 2
        bc[st, b + 1] = jnp.where(moved, br[st, b], bc[st, b])

    def gather_first(st):
        collect(st)
        go(sends(st, (0, 1, 2, 3) if st in PASSED else (6, 3, 4, 5, 1, 2, 0)))

    def gather_side(st):
        arrive(arrivals(st, (0,)))
        go(sends(st, (6, 4, 5)))

    def gather_last(st):
        arrive(arrivals(st, range(1 if st in PASSED else 0, 7)))
        multiply(st)

    def mirror(st, b):
        if b == 0:
            if st == 0:
                load_pair.wait()
            bc[st, 0] = x_take(st)
        else:
            b_take(st, b - 1)
        if b < 3:
            go([b_copy(st, b)])

    table = {
        "f": gather_first, "s": gather_side, "l": gather_last, "x": x_go,
        "m": z_mid,
        "a": functools.partial(mirror, b=0), "b": functools.partial(mirror, b=1),
        "c": functools.partial(mirror, b=2), "d": functools.partial(mirror, b=3),
    }
    for step in (
        "f0", "s0", "f1", "s1", "l0", "f2", "m0", "l1", "f3", "l2",
        "m1", "x0", "l3", "m2", "x1", "a0", "m3", "a1", "x2", "b0",
        "b1", "x3", "c0", "c1", "d0", "d1",
    ):
        table[step[0]](int(step[1]))
    halves = [x_take(2 + h) - bc[h, 3] for h in range(2)]
    for m in range(BLOCKS // 2):
        cols = slice(m * BW, (m + 1) * BW)
        pair = interleave(halves[0][:, cols], halves[1][:, cols])
        for n in range(2):
            out_ref[:, (2 * m + n) * BW:(2 * m + n + 1) * BW] = pair[n]

    for st in range(STREAMS):
        spread_wait(st)
    for copy in started:
        copy.wait_send()


def shards(
    amplitudes, piece_len, ladder_tiles, cycle_tiles, tile_owner, tile_piece, tile_block, pair_map
):
    vmem, anywhere = pl.BlockSpec(memory_space=pltpu.VMEM), pl.BlockSpec(memory_space=pltpu.HBM)
    dma = pltpu.SemaphoreType.DMA
    return pl.pallas_call(
        kernel,
        out_shape=jax.ShapeDtypeStruct((BR, COLS), F32),
        in_specs=[anywhere] * 8,
        out_specs=vmem,
        scratch_shapes=[
            pltpu.VMEM((3, 8, N_BLK * TILES // 8), I32),
            pltpu.SMEM((N_GRP, N_BLK), I32),
            pltpu.SMEM((PIECES,), I32),
            pltpu.VMEM((2, TILES, SL, BW), F32),
            pltpu.VMEM((TILES * PK, 2 * BW), BF16),
            pltpu.VMEM((STREAMS, N_BLK * SLOT_ROWS, BW), F32),
            pltpu.VMEM((STREAMS, N_BLK * SLOT_ROWS, BW), F32),
            pltpu.VMEM((STREAMS, PIECES, TW, SC), F32),
            pltpu.VMEM((KD, SC), BF16),
            pltpu.VMEM((KD, SC), BF16),
            pltpu.VMEM((ROWS * PIECES, TW), F32),
            pltpu.VMEM((2, ROWS // 2, KD), BF16),
            pltpu.VMEM((2, ROWS // 2, KD), BF16),
            pltpu.VMEM((STREAMS, ROWS // 2, SC), F32),
            pltpu.VMEM((STREAMS, ROWS // 2, SC), F32),
            pltpu.VMEM((STREAMS, ROWS // 2, SC), F32),
            pltpu.VMEM((STREAMS, 2, 2, 4, BR, SC), F32),
            pltpu.VMEM((STREAMS, BR, SC), F32),
            pltpu.VMEM((2, 4, BR, SC), F32),
            pltpu.VMEM((2, 3, BR, SC), F32),
            pltpu.VMEM((PIECES * BLOCKS * PK, N_BLK * SLOT_ROWS), BF16),
            dma((8,)),
            dma((STREAMS,)),
            dma((STREAMS,)),
            dma((STREAMS, 9)),
            dma((STREAMS, 9)),
            dma((STREAMS, 2)),
            dma((STREAMS, 2)),
            dma((STREAMS, 2, 2, 4)),
            dma((STREAMS, 2, 2, 4)),
            dma((STREAMS,)),
            dma((STREAMS,)),
            dma((2, 3)),
            dma((2, 3)),
        ],
        compiler_params=pltpu.CompilerParams(
            collective_id=0, has_side_effects=True, vmem_limit_bytes=60 * 1024 * 1024
        ),
    )(
        tile_owner.reshape(8, -1), tile_piece.reshape(8, -1), tile_block.reshape(8, -1), pair_map, piece_len,
        amplitudes.reshape(ROWS * PIECES, TW), ladder_tiles, cycle_tiles,
    )


def solution(mesh):
    placed = (
        P("grp", "blk", None),
        P("blk"),
        P("blk", None, None),
        P("blk", None, None),
        P(),
        P(),
        P(),
        P(),
    )
    return jax.shard_map(
        shards, mesh=mesh, in_specs=placed, out_specs=P(("grp", "blk"), None), check_vma=False
    )
```

```python
import functools

import jax
import jax.numpy as jnp
from jax import lax
from jax.experimental import pallas as pl
from jax.experimental.pallas import tpu as pltpu
from jax.sharding import PartitionSpec as P

BLOCKS = 4
PAIR_CAP = 2
F32 = jnp.float32
BF16 = jnp.bfloat16
I32 = jnp.int32

NZ = 8
NY = 4
N_BLK = 32
N_GRP = 8
TILES = 32
TW = 128
BW = 128
PIECES = 4
FIRST = 2
PASSED = (0, 1)
STREAMS = 4
HALF = BW // 2
SL = TW // N_GRP
PK = SL // 2
SLOT_ROWS = PAIR_CAP * PK
ROWS = 1024
BR = ROWS // N_BLK
KD = PIECES * TW
COLS = BLOCKS * BW
SC = COLS // 2


def iota(shape, dim):
    return lax.broadcasted_iota(I32, shape, dim)


def split2(x):
    hi = x.astype(BF16)
    lo = (x - hi.astype(F32)).astype(BF16)
    return hi, lo


def interleave(a, b):
    left = lax.broadcasted_iota(I32, a.shape, 1) < HALF
    return jnp.where(left, a, pltpu.roll(b, HALF, 1)), jnp.where(left, pltpu.roll(a, HALF, 1), b)


def dot(a, b):
    return jnp.dot(a, b, preferred_element_type=F32)


def kernel(
    owner_hbm, piece_hbm, block_hbm, pair_hbm, plen_hbm, amp_hbm, lad_hbm, cyc_hbm, out_ref,
    maps, pair_ref, plen_ref, tl, cat, send, recv, w2, wh, wl, amp, ah, al, ps, po, pr, zr, xr, bc, br, kd,
    local_sem, a2a_send, a2a_recv, ag_send, ag_recv, core_send, core_recv,
    z_send, z_recv, x_send, x_recv, b_send, b_recv,
):
    me = lax.axis_index("blk")
    g = lax.axis_index("grp")
    z, xh, core = me // 4, (me // 2) % 2, me % 2
    y, xl = g // 2, g % 2

    def xor_grp(bit):
        return g + bit - 2 * bit * ((g // bit) % 2)

    def xor_blk(bit):
        return me + bit - 2 * bit * ((me // bit) % 2)

    def at_grp(dy, flip):
        return ((y + dy + NY) % NY) * 2 + (xl + flip) % 2

    def at_z(dz):
        return ((z + dz + NZ) % NZ) * 4 + me % 4

    rows = pl.ds(pl.multiple_of(g * SL, SL), SL)
    load_c = pltpu.make_async_copy(cyc_hbm.at[:, rows, :], tl.at[0], local_sem.at[0])
    load_l = pltpu.make_async_copy(lad_hbm.at[:, rows, :], tl.at[1], local_sem.at[1])
    load_a = pltpu.make_async_copy(amp_hbm, amp, local_sem.at[2])
    maps_in = [
        pltpu.make_async_copy(ref, maps.at[n], local_sem.at[3 + n])
        for n, ref in enumerate((owner_hbm, piece_hbm, block_hbm))
    ]
    load_pair = pltpu.make_async_copy(pair_hbm, pair_ref, local_sem.at[6])
    load_plen = pltpu.make_async_copy(plen_hbm, plen_ref, local_sem.at[7])
    for copy in maps_in:
        copy.start()
    load_c.start()
    load_l.start()
    load_plen.start()
    load_a.start()
    load_pair.start()
    started = []

    barrier = pltpu.get_barrier_semaphore()

    def greet(k, carry):
        pl.semaphore_signal(barrier, inc=1, device_id={"blk": (me + k) % N_BLK})
        return carry

    lax.fori_loop(1, N_BLK, greet, 0)
    for peer in [at_grp(dy, dx) for dy in range(4) for dx in range(2) if dy or dx]:
        pl.semaphore_signal(barrier, inc=1, device_id={"grp": peer})

    for copy in maps_in:
        copy.wait()
    lanes = N_BLK * TILES // 8
    per = lanes // TILES
    repeat = jnp.where(iota((N_BLK, 8), 0) // per == iota((N_BLK, 8), 1), 1.0, 0.0).astype(BF16)
    fold = jnp.where(iota((lanes, TILES), 0) % TILES == iota((lanes, TILES), 1), 1.0, 0.0).astype(BF16)
    mine = iota((N_BLK, lanes), 1) // TILES == iota((N_BLK, lanes), 0) % per

    def unfold(values):
        wide = jnp.where(mine, dot(repeat, values.astype(F32).astype(BF16)), 0.0)
        return dot(wide.astype(BF16), fold)

    owners = unfold(maps[0])
    keys = unfold(maps[1] * BLOCKS + maps[2])

    me_f = me.astype(F32)
    own_r = jnp.sum(jnp.where(iota((N_BLK, TILES), 0) == me, owners, 0.0), axis=0, keepdims=True)
    square = (TILES, TILES)
    own_c = jnp.sum(jnp.where(iota(square, 0) == iota(square, 1), own_r, 0.0), axis=1, keepdims=True)
    same = jnp.where((own_c == own_r) & (iota(square, 0) < iota(square, 1)), 1.0, 0.0)
    slot = own_r * PAIR_CAP + jnp.sum(same, axis=0, keepdims=True)
    width = TILES * PK
    expand = jnp.where(iota((TILES, width), 1) // PK == iota((TILES, width), 0), 1.0, 0.0)
    slot8 = jnp.broadcast_to(slot, (8, TILES))
    slot_l = dot(slot8.astype(BF16), expand.astype(BF16))[0:1, :].astype(I32)
    goal = slot_l * PK + iota((1, width), 1) % PK

    def fill(st):
        tiles = tl[st // 2]
        packed = interleave(tiles[:, :PK, :].reshape(width, BW), tiles[:, PK:, :].reshape(width, BW))
        hi, lo = split2(packed[st % 2])
        cat[:, :BW] = hi
        cat[:, BW:] = lo

        def block(b, carry):
            onehot = jnp.where(iota((128, width), 0) + b * 128 == goal, 1.0, 0.0).astype(BF16)
            both = dot(onehot, cat[...])
            send[st, pl.ds(pl.multiple_of(b * 128, 128), 128), :] = both[:, :BW] + both[:, BW:]
            return carry

        lax.fori_loop(0, N_BLK * SLOT_ROWS // 128, block, 0)

    def slot_rows(device):
        return pl.ds(pl.multiple_of(device * SLOT_ROWS, SLOT_ROWS), SLOT_ROWS)

    def spread_all(st):
        for hop_x in (1, 0):
            for hop_core in (0, 1):
                for hop in (4, 3, -3, 2, -2, 1, -1, 0):
                    if not (hop or hop_x or hop_core):
                        continue
                    to = (z + hop + NZ) % NZ * 4 + (xh + hop_x) % 2 * 2 + (core + hop_core) % 2
                    pltpu.make_async_remote_copy(
                        src_ref=send.at[st, slot_rows(to), :],
                        dst_ref=recv.at[st, slot_rows(me), :],
                        send_sem=a2a_send.at[st],
                        recv_sem=a2a_recv.at[st],
                        device_id={"blk": to},
                    ).start()

    def spread_wait(st):
        part = send.at[st, pl.ds(0, (N_BLK - 1) * SLOT_ROWS), :]
        pltpu.make_async_copy(part, part, a2a_send.at[st]).wait()

    def keep(st):
        recv[st, slot_rows(me), :] = send[st, slot_rows(me), :]

    def a2a_all(st):
        part = recv.at[st, pl.ds(0, (N_BLK - 1) * SLOT_ROWS), :]
        return pltpu.make_async_copy(part, part, a2a_recv.at[st])

    load_c.wait()
    fill(0)
    keep(0)
    pl.semaphore_wait(barrier, N_BLK - 1 + 7)
    spread_all(0)
    fill(1)
    keep(1)
    spread_all(1)
    load_l.wait()
    for st in (2, 3):
        fill(st)
        keep(st)
        spread_all(st)

    hits = jnp.where(owners == me_f, 1.0, 0.0)
    tri = jnp.where(iota(square, 0) < iota(square, 1), 1.0, 0.0)
    before = dot(hits.astype(BF16), tri.astype(BF16))
    depth = N_BLK * SLOT_ROWS
    place = iota((N_BLK, depth), 1) // PK - iota((N_BLK, depth), 0) * PAIR_CAP
    key_l = jnp.zeros((1, depth), F32)
    for k in range(PAIR_CAP):
        chosen = jnp.where(before == float(k), hits, 0.0)
        found = jnp.sum(chosen, axis=1, keepdims=True)
        where = jnp.sum(chosen * keys, axis=1, keepdims=True) + 64.0 * (1.0 - found)
        key_l += jnp.sum(jnp.where(place == k, where, 0.0), axis=0, keepdims=True)
    goal_d = key_l.astype(I32) * PK + iota((1, depth), 1) % PK
    kd[...] = jnp.where(iota((PIECES * BLOCKS * PK, depth), 0) == goal_d, 1.0, 0.0).astype(BF16)

    def prepare(t, carry):
        source = (z + FIRST + t // 2 + NZ) % NZ * 2 + t % 2
        for half in range(2):
            for p in range(PIECES):
                start = (source * 2 * BR + half * BR) * PIECES + p
                v = amp[pl.ds(start, BR, stride=PIECES), :]
                v = jnp.where(iota((BR, TW), 1) < plen_ref[p], v, 0.0)
                hi, lo = split2(v)
                r = pl.ds(pl.multiple_of(t * BR, BR), BR)
                ah[half, r, p * TW:(p + 1) * TW] = hi
                al[half, r, p * TW:(p + 1) * TW] = lo
        return carry

    load_a.wait()
    load_plen.wait()
    lax.fori_loop(0, N_BLK // 2, prepare, 0)

    def collect(st):
        a2a_all(st).wait()
        hi, lo = split2(recv[st])
        total = dot(kd[...], hi) + dot(kd[...], lo)
        for q in range(PIECES):
            for m in range(BLOCKS // 2):
                at = (q * BLOCKS + 2 * m) * PK
                part = jnp.concatenate(interleave(total[at:at + PK, :], total[at + PK:at + 2 * PK, :]), axis=0)
                cols = pl.ds(m * BW, BW)
                if st >= 2:
                    part = part + 2.0 * w2[st - 2, q, rows, cols]
                w2[st, q, rows, cols] = part

    def gather_copy(st, n, owner, to):
        at = pl.ds(pl.multiple_of(owner * SL, SL), SL)
        ref = w2.at[st, :, at, :]
        return pltpu.make_async_remote_copy(
            src_ref=ref, dst_ref=ref, send_sem=ag_send.at[st, n], recv_sem=ag_recv.at[st, n],
            device_id={"grp": to},
        )

    up, down, over, side = at_grp(1, 0), at_grp(-1, 0), at_grp(2, 0), at_grp(0, 1)
    up_side, down_side, over_side = at_grp(1, 1), at_grp(-1, 1), at_grp(2, 1)

    def sends(st, ns):
        table = {0: (g, side), 1: (g, up), 2: (g, down), 3: (g, over)}
        if st in PASSED:
            table.update({4: (side, up), 5: (side, down), 6: (side, over)})
        else:
            table.update({4: (g, up_side), 5: (g, down_side), 6: (g, over_side)})
        return [gather_copy(st, n, *table[n]) for n in ns]

    def arrivals(st, ns):
        table = {0: side, 1: down, 2: up, 3: over, 4: down_side, 5: up_side, 6: over_side}
        return [gather_copy(st, n, table[n], side) for n in ns]

    def go(copies):
        for copy in copies:
            copy.start()
            started.append(copy)

    def arrive(copies):
        for copy in copies:
            copy.wait_recv()

    def widen(st):
        for q in range(PIECES):
            hi, lo = split2(w2[st, q])
            wh[q * TW:(q + 1) * TW, :] = hi
            wl[q * TW:(q + 1) * TW, :] = lo

    def product(st, half, dst, part):
        r = pl.ds(part * 256, 256)
        a, b = ah[half, r, :], al[half, r, :]
        dst[st, r, :] = dot(a, wh[...]) + (dot(a, wl[...]) + dot(b, wh[...]))

    def core_copy(st, part):
        r = pl.ds(part * 256, 256)
        return pltpu.make_async_remote_copy(
            src_ref=ps.at[st, r, :], dst_ref=pr.at[st, r, :],
            send_sem=core_send.at[st, part], recv_sem=core_recv.at[st, part],
            device_id={"blk": xor_blk(1)},
        )

    def core_add(st, part):
        core_copy(st, part).wait_recv()

        def one(i, carry):
            r = pl.ds(pl.multiple_of(part * 256 + i * 64, 64), 64)
            po[st, r, :] += pr[st, r, :]
            return carry

        lax.fori_loop(0, 4, one, 0)

    def multiply(st):
        widen(st)
        product(st, 1 - core, ps, 0)
        go([core_copy(st, 0)])
        product(st, 1 - core, ps, 1)
        go([core_copy(st, 1)])
        product(st, core, po, 0)
        core_add(st, 0)
        z_far(st)
        product(st, core, po, 1)
        core_add(st, 1)
        z_near(st)

    def chunk(distance, half):
        return pl.ds(((distance - FIRST) % NZ * 2 + half) * BR, BR)

    def z_copy(st, way, half, distance):
        sign = 1 - 2 * way
        return pltpu.make_async_remote_copy(
            src_ref=po.at[st, chunk(sign * distance, half), :], dst_ref=zr.at[st, way, half, distance - 1],
            send_sem=z_send.at[st, way, half, distance - 1], recv_sem=z_recv.at[st, way, half, distance - 1],
            device_id={"blk": at_z(sign * (1 if distance % 2 else 2))},
        )

    def z_far(st):
        for way in range(2):
            go([z_copy(st, way, way, 4)])
        for half in range(2):
            for way in range(2):
                go([z_copy(st, way, half, 3)])

    def z_near(st):
        for half in range(2):
            for way in range(2):
                go([z_copy(st, way, half, 1)])

    def z_mid(st):
        for lead in (1, 0):
            for way in range(2):
                half = way if lead == 0 else 1 - way
                z_copy(st, way, half, 3).wait_recv()
                total = po[st, chunk(2 - 4 * way, half), :] + zr[st, way, half, 2]
                if lead == 0:
                    z_copy(st, way, half, 4).wait_recv()
                    total = total + zr[st, way, half, 3]
                po[st, chunk(2 - 4 * way, half), :] = total
                go([z_copy(st, way, half, 2)])

    def own_rows(half):
        return pl.ds(pl.multiple_of(((NZ - FIRST) * 2 + half) * BR, BR), BR)

    def x_copy(st):
        return pltpu.make_async_remote_copy(
            src_ref=po.at[st, own_rows(1 - xh), :], dst_ref=xr.at[st],
            send_sem=x_send.at[st], recv_sem=x_recv.at[st], device_id={"blk": xor_blk(2)},
        )

    def finish(st, half):
        for distance in (1, 2):
            for way in range(2):
                part = zr.at[st, way, half, distance - 1]
                pltpu.make_async_copy(part, part, z_recv.at[st, way, half, distance - 1]).wait()
        near = zr[st, 0, half, 0] + zr[st, 1, half, 0]
        po[st, own_rows(half), :] += near + (zr[st, 0, half, 1] + zr[st, 1, half, 1])

    def x_go(st):
        finish(st, 1 - xh)
        go([x_copy(st)])
        finish(st, xh)

    def x_take(st):
        x_copy(st).wait_recv()
        return po[st, own_rows(xh), :] + xr[st]

    def b_copy(st, b):
        return pltpu.make_async_remote_copy(
            src_ref=bc.at[st, b], dst_ref=br.at[st, b], send_sem=b_send.at[st, b], recv_sem=b_recv.at[st, b],
            device_id={"grp": xor_grp(1 << b)},
        )

    def b_take(st, b):
        b_copy(st, b).wait_recv()
        moved = (pair_ref[g, me] // (1 << b)) % 2 != (g // (1 << b)) % 2
        bc[st, b + 1] = jnp.where(moved, br[st, b], bc[st, b])

    def gather_first(st):
        collect(st)
        go(sends(st, (0, 1, 2, 3) if st in PASSED else (6, 3, 4, 5, 1, 2, 0)))

    def gather_side(st):
        arrive(arrivals(st, (0,)))
        go(sends(st, (6, 4, 5)))

    def gather_last(st):
        arrive(arrivals(st, range(1 if st in PASSED else 0, 7)))
        multiply(st)

    def mirror(st, b):
        if b == 0:
            if st == 0:
                load_pair.wait()
            bc[st, 0] = x_take(st)
        else:
            b_take(st, b - 1)
        if b < 3:
            go([b_copy(st, b)])

    def drain(_):
        for st in range(STREAMS):
            spread_wait(st)
        for copy in started[:-3]:
            copy.wait_send()
        del started[:-3]

    table = {
        "w": drain, "f": gather_first, "s": gather_side, "l": gather_last, "x": x_go,
        "m": z_mid,
        "a": functools.partial(mirror, b=0), "b": functools.partial(mirror, b=1),
        "c": functools.partial(mirror, b=2), "d": functools.partial(mirror, b=3),
    }
    for step in (
        "f0", "s0", "f1", "s1", "l0", "f2", "m0", "l1", "f3", "l2",
        "m1", "x0", "l3", "m2", "x1", "a0", "m3", "a1", "x2", "b0",
        "b1", "x3", "c0", "c1", "w0", "d0", "d1",
    ):
        table[step[0]](int(step[1]))
    halves = [x_take(2 + h) - bc[h, 3] for h in range(2)]
    for m in range(BLOCKS // 2):
        cols = slice(m * BW, (m + 1) * BW)
        pair = interleave(halves[0][:, cols], halves[1][:, cols])
        for n in range(2):
            out_ref[:, (2 * m + n) * BW:(2 * m + n + 1) * BW] = pair[n]

    for copy in started:
        copy.wait_send()


def shards(
    amplitudes, piece_len, ladder_tiles, cycle_tiles, tile_owner, tile_piece, tile_block, pair_map
):
    vmem, anywhere = pl.BlockSpec(memory_space=pltpu.VMEM), pl.BlockSpec(memory_space=pltpu.HBM)
    dma = pltpu.SemaphoreType.DMA
    return pl.pallas_call(
        kernel,
        out_shape=jax.ShapeDtypeStruct((BR, COLS), F32),
        in_specs=[anywhere] * 8,
        out_specs=vmem,
        scratch_shapes=[
            pltpu.VMEM((3, 8, N_BLK * TILES // 8), I32),
            pltpu.SMEM((N_GRP, N_BLK), I32),
            pltpu.SMEM((PIECES,), I32),
            pltpu.VMEM((2, TILES, SL, BW), F32),
            pltpu.VMEM((TILES * PK, 2 * BW), BF16),
            pltpu.VMEM((STREAMS, N_BLK * SLOT_ROWS, BW), F32),
            pltpu.VMEM((STREAMS, N_BLK * SLOT_ROWS, BW), F32),
            pltpu.VMEM((STREAMS, PIECES, TW, SC), F32),
            pltpu.VMEM((KD, SC), BF16),
            pltpu.VMEM((KD, SC), BF16),
            pltpu.VMEM((ROWS * PIECES, TW), F32),
            pltpu.VMEM((2, ROWS // 2, KD), BF16),
            pltpu.VMEM((2, ROWS // 2, KD), BF16),
            pltpu.VMEM((STREAMS, ROWS // 2, SC), F32),
            pltpu.VMEM((STREAMS, ROWS // 2, SC), F32),
            pltpu.VMEM((STREAMS, ROWS // 2, SC), F32),
            pltpu.VMEM((STREAMS, 2, 2, 4, BR, SC), F32),
            pltpu.VMEM((STREAMS, BR, SC), F32),
            pltpu.VMEM((2, 4, BR, SC), F32),
            pltpu.VMEM((2, 3, BR, SC), F32),
            pltpu.VMEM((PIECES * BLOCKS * PK, N_BLK * SLOT_ROWS), BF16),
            dma((8,)),
            dma((STREAMS,)),
            dma((STREAMS,)),
            dma((STREAMS, 9)),
            dma((STREAMS, 9)),
            dma((STREAMS, 2)),
            dma((STREAMS, 2)),
            dma((STREAMS, 2, 2, 4)),
            dma((STREAMS, 2, 2, 4)),
            dma((STREAMS,)),
            dma((STREAMS,)),
            dma((2, 3)),
            dma((2, 3)),
        ],
        compiler_params=pltpu.CompilerParams(
            collective_id=0, has_side_effects=True, vmem_limit_bytes=60 * 1024 * 1024
        ),
    )(
        tile_owner.reshape(8, -1), tile_piece.reshape(8, -1), tile_block.reshape(8, -1), pair_map, piece_len,
        amplitudes.reshape(ROWS * PIECES, TW), ladder_tiles, cycle_tiles,
    )


def solution(mesh):
    placed = (
        P("grp", "blk", None),
        P("blk"),
        P("blk", None, None),
        P("blk", None, None),
        P(),
        P(),
        P(),
        P(),
    )
    return jax.shard_map(
        shards, mesh=mesh, in_specs=placed, out_specs=P(("grp", "blk"), None), check_vma=False
    )
```
